512 devices in a mesh: tm: 32 (over y, z_lo, core), space: 16 (over x, z_hi).
Axes of the slice: x: 4, y: 4, z: 16 (z_hi: 4, z_lo: 4; z = z_hi * 4 + z_lo), core: 2. Of those that a mesh axis runs over, the one named last changes fastest.
Arguments:
- old_nodes: float32 [32, 5, 4, 96, 8, 128], P('tm', None, None, 'space'), may hold values from -6 to 6
- initial: float32 [4, 96, 8, 128], P(None, 'space'), may hold values from -6 to 6
- shear_modulus: float32 [96, 8, 128], P('space'), may hold values from 0.2 to 1
- mobility: float32 [96, 8, 128], P('space'), may hold values from 0.2 to 1
Outputs:
- new_nodes: float32 [32, 5, 4, 96, 8, 128], P('tm', None, None, 'space')
- next_start: float32 [32, 4, 96, 8, 128], P('tm', None, 'space')
The draws below stay inside these ranges and needn't reach their ends.
All inputs are finite; a program needn't handle non-finite values.
Results may differ from the reference program's by a relative error of at most 0.00002.
Values sent between devices are 32-bit elements; how exact they have to be, the bound alone decides.
A program may use at most 64 MiB of HBM per device.

```python
import math
import jax
import jax.numpy as jnp
from jax import lax

NX = 8
NY = 128
NODES = 5
COMPS = 4
NZ = 96
SLICES = 32


def levels(stream_key, dims, split, low, top_value):
    def one(dim, shards_of):
        heights = jax.random.uniform(jax.random.fold_in(jax.random.fold_in(stream_key, 6), dim), (shards_of,), jnp.float32, low / len(split), top_value / len(split))
        return jnp.repeat(jnp.exp(heights), dims[dim] // shards_of).reshape((-1,) + (1,) * (len(dims) - dim - 1))

    factor_of = one(*split[0])
    for cut in split[1:]:
        factor_of = factor_of * one(*cut)
    return factor_of


def scatter_about(rng, dims, width, most, split=(), kind=jnp.bfloat16):
    entries = width * jax.random.normal(rng, dims, jnp.float32)
    if split:
        entries = entries * levels(rng, dims, split, -0.22, 0.18)
    return jnp.clip(entries, -most, most).astype(kind)


def setup_inputs(seed: int = 0) -> dict:
    keys = jax.random.split(jax.random.key(seed), 5)
    old_nodes = scatter_about(keys[0], (SLICES, NODES, COMPS, NZ, NX, NY), 1.0, 6.0, ((0, 32), (3, 16)), jnp.float32)
    initial = scatter_about(keys[1], (COMPS, NZ, NX, NY), 1.0, 6.0, ((1, 16),), jnp.float32)
    shear_modulus = jnp.clip(jnp.exp(math.log(1.0) - 1.609438 * jax.random.uniform(keys[2], (NZ, NX, NY), jnp.float32) ** levels(keys[2], (NZ, NX, NY), ((0, 16),), -0.2, 0.2)), 0.2, 1.0)
    mobility = jnp.clip(jnp.exp(math.log(1.0) - 1.609438 * jax.random.uniform(keys[3], (NZ, NX, NY), jnp.float32) ** levels(keys[3], (NZ, NX, NY), ((0, 16),), -0.2, 0.2)), 0.2, 1.0)
    return {"old_nodes": old_nodes, "initial": initial, "shear_modulus": shear_modulus, "mobility": mobility}


coupling = 0.5
slice_step = 0.4

def node_tables():
    root_gap = math.sqrt(3.0 / 7.0)
    points = [0.0, (1.0 - root_gap) / 2.0, 0.5, (1.0 + root_gap) / 2.0, 1.0]
    polys = []
    for node in range(5):
        coeffs = [1.0]
        for other in range(5):
            if other != node:
                denom = points[node] - points[other]
                grown = [0.0] * (len(coeffs) + 1)
                for power in range(len(coeffs)):
                    grown[power + 1] += coeffs[power] / denom
                    grown[power] -= points[other] * coeffs[power] / denom
                coeffs = grown
        polys.append(coeffs)
    integral = []
    for column in range(4):
        lower = points[column]
        upper = points[column + 1]
        table_row = []
        for node in range(5):
            total = 0.0
            for power in range(5):
                total += polys[node][power] * (upper ** (power + 1) - lower ** (power + 1)) / (power + 1)
            table_row.append(total * slice_step)
        integral.append(table_row)
    widths = [(points[column + 1] - points[column]) * slice_step for column in range(4)]
    return (integral, widths)

def component(source, number):
    return source[..., number, :, :, :]

def operator(padz, stiffness, fluidity, lap_scale, grad_scale):
    padded = jnp.pad(padz, [(0, 0)] * (padz.ndim - 2) + [(1, 1), (1, 1)])
    center = padded[..., 1:-1, 1:-1, 1:-1]
    z_plus = padded[..., 2:, 1:-1, 1:-1]
    z_minus = padded[..., :-2, 1:-1, 1:-1]
    x_plus = padded[..., 1:-1, 2:, 1:-1]
    x_minus = padded[..., 1:-1, :-2, 1:-1]
    y_plus = padded[..., 1:-1, 1:-1, 2:]
    y_minus = padded[..., 1:-1, 1:-1, :-2]
    laplace = (z_plus + z_minus + x_plus + x_minus + y_plus + y_minus - 6.0 * center) * lap_scale
    grad_z = (component(z_plus, 3) - component(z_minus, 3)) * grad_scale
    grad_x = (component(x_plus, 3) - component(x_minus, 3)) * grad_scale
    grad_y = (component(y_plus, 3) - component(y_minus, 3)) * grad_scale
    diverge = (component(z_plus, 0) - component(z_minus, 0) + component(x_plus, 1) - component(x_minus, 1) + component(y_plus, 2) - component(y_minus, 2)) * grad_scale
    return jnp.stack([stiffness * component(laplace, 0) - coupling * grad_z, stiffness * component(laplace, 1) - coupling * grad_x, stiffness * component(laplace, 2) - coupling * grad_y, fluidity * component(laplace, 3) - coupling * diverge], axis=-4)

def pad_depth(source):
    return jnp.pad(source, [(0, 0)] * (source.ndim - 3) + [(1, 1), (0, 0), (0, 0)])

def restrict(source):
    new_shape = source.shape[:-3] + (source.shape[-3] // 2, 2, source.shape[-2] // 2, 2, source.shape[-1] // 2, 2)
    return lax.optimization_barrier(jnp.mean(source.reshape(new_shape), axis=(-5, -3, -1)))

def prolong(source):
    return jnp.repeat(jnp.repeat(jnp.repeat(source, 2, -3), 2, -2), 2, -1)

def spread_sum(table_row, images):
    total = table_row[0] * images[0:1]
    for position in range(1, 5):
        total = total + table_row[position] * images[position:position + 1]
    return total

def slice_iteration(old_here, start_value, shear_modulus, mobility):
    integral, widths = node_tables()

    def evaluate(source):
        return operator(pad_depth(source), shear_modulus, mobility, 1.0, 0.5)
    old_f = evaluate(old_here)
    current = start_value
    f_current = evaluate(start_value)
    values = [current]
    images = []
    for column in range(4):
        advanced = current + widths[column] * (f_current - old_f[column:column + 1]) + spread_sum(integral[column], old_f)
        images.append(f_current)
        values.append(advanced)
        current = advanced
        f_current = evaluate(advanced)
    images.append(f_current)
    fine_f = jnp.concatenate(images, axis=0)
    coarse_nodes = restrict(jnp.concatenate(values, axis=0))
    coarse_shear = restrict(shear_modulus)
    coarse_mobility = restrict(mobility)

    def coarse_eval(source):
        return operator(pad_depth(source), coarse_shear, coarse_mobility, 0.25, 0.25)
    coarse_old = coarse_eval(coarse_nodes[1:4])
    restricted = [restrict(spread_sum(integral[column], fine_f)) for column in range(4)]
    coarse_values = [coarse_nodes[0:1]]
    coarse_values.append(coarse_values[0] + restricted[0])
    for column in range(1, 4):
        now_value = coarse_values[column]
        coarse_values.append(now_value + widths[column] * (coarse_eval(now_value) - coarse_old[column - 1:column]) + restricted[column])
    result = [start_value]
    for column in range(1, 5):
        result.append(values[column] + prolong(coarse_values[column] - coarse_nodes[column:column + 1]))
    return jnp.concatenate(result, axis=0)

def reference(old_nodes, initial, shear_modulus, mobility):
    starts = jnp.concatenate([initial[None], old_nodes[:-1, 4]], axis=0)

    def one_slice(slice_pair):
        return slice_iteration(slice_pair[0], slice_pair[1][None], shear_modulus, mobility)
    new_nodes = lax.map(one_slice, (old_nodes, starts))
    next_start = jnp.concatenate([initial[None], new_nodes[:-1, 4]], axis=0)
    return (new_nodes, next_start)
```

```python
import functools
import math

import jax
import jax.numpy as jnp
from jax import lax
from jax.experimental import pallas as pl
from jax.experimental.pallas import tpu as pltpu
from jax.sharding import PartitionSpec as P

MESH = pl.DeviceIdType.MESH
slice_step = 0.4
LAYERS = 6
EXT = 12
FIELD = 4


def node_tables():
    root_gap = math.sqrt(3.0 / 7.0)
    points = [0.0, (1.0 - root_gap) / 2.0, 0.5, (1.0 + root_gap) / 2.0, 1.0]
    polys = []
    for node in range(5):
        coeffs = [1.0]
        for other in range(5):
            if other != node:
                denom = points[node] - points[other]
                grown = [0.0] * (len(coeffs) + 1)
                for power in range(len(coeffs)):
                    grown[power + 1] += coeffs[power] / denom
                    grown[power] -= points[other] * coeffs[power] / denom
                coeffs = grown
        polys.append(coeffs)
    integral = []
    for column in range(4):
        lower = points[column]
        upper = points[column + 1]
        table_row = []
        for node in range(5):
            total = 0.0
            for power in range(5):
                total += (
                    polys[node][power] * (upper ** (power + 1) - lower ** (power + 1)) / (power + 1)
                )
            table_row.append(total * slice_step)
        integral.append(table_row)
    widths = [(points[column + 1] - points[column]) * slice_step for column in range(4)]
    return (integral, widths)


def positions(shape, axis):
    return lax.broadcasted_iota(jnp.int32, shape, axis)


def at(value, axis, step):
    size = value.shape[axis]
    moved = pltpu.roll(value, (-step) % size, axis)
    where = positions(value.shape, axis)
    inside = where < size - step if step > 0 else where >= -step
    return jnp.where(inside, moved, 0.0)


def operator(q, stiff, fluid, grad, step):
    out = [None] * 4
    diverge = None
    for k in (3, 0, 1, 2):
        center, below, above = q[k][1:-1], q[k][:-2], q[k][2:]
        xp, xm = at(center, 1, step), at(center, 1, -step)
        yp, ym = at(center, 2, step), at(center, 2, -step)
        laplace = ((xp + xm) + (yp + ym)) + (above + below) - 6.0 * center
        if k == 3:
            flow = fluid * laplace
            grads = [grad * (above - below), grad * (xp - xm), grad * (yp - ym)]
        else:
            out[k] = stiff * laplace - grads[k]
            part = (above - below, xp - xm, yp - ym)[k]
            diverge = part if diverge is None else diverge + part
    out[3] = flow - grad * diverge
    return out


def from_below(q, stiff, fluid, grad):
    return [stiff * q[0] + grad * q[3], stiff * q[1], stiff * q[2], fluid * q[3] + grad * q[0]]


def from_above(q, stiff, fluid, grad):
    return [stiff * q[0] - grad * q[3], stiff * q[1], stiff * q[2], fluid * q[3] - grad * q[0]]


def even(shape, axis):
    return positions(shape, axis) % 2 == 0


def pair_sums(a, b, axis):
    size = a.shape[axis]
    is_even = even(a.shape, axis)
    kept, other = jnp.where(is_even, a, b), jnp.where(is_even, b, a)
    return kept + jnp.where(is_even, pltpu.roll(other, size - 1, axis), pltpu.roll(other, 1, axis))


def means(q):
    return 0.125 * pair_sums(pair_sums(q[0], q[1], 2), pair_sums(q[2], q[3], 2), 1)


def layer_pairs(v):
    return jnp.concatenate([v[2 * i : 2 * i + 1] + v[2 * i + 1 : 2 * i + 2] for i in range(3)], axis=0)


def woven(q):
    shape = q[0].shape
    ye, xe = even(shape, 2), even(shape, 1)
    return jnp.where(xe, jnp.where(ye, q[0], q[1]), jnp.where(ye, q[2], q[3]))


def spread(p):
    ye, xe = even(p.shape, 2), even(p.shape, 1)
    a = jnp.where(ye, p, pltpu.roll(p, 1, 2))
    b = jnp.where(ye, pltpu.roll(p, 127, 2), p)
    return [
        jnp.where(xe, a, pltpu.roll(a, 1, 1)),
        jnp.where(xe, b, pltpu.roll(b, 1, 1)),
        jnp.where(xe, pltpu.roll(a, 7, 1), a),
        jnp.where(xe, pltpu.roll(b, 7, 1), b),
    ]


def twice(v):
    return jnp.concatenate([v[i // 2 : i // 2 + 1] for i in range(LAYERS)], axis=0)


def ends(v, low, high):
    return jnp.concatenate([v[:1] + low, v[1:-1], v[-1:] + high], axis=0)


def padded(v):
    zero = jnp.zeros_like(v[:1])
    return jnp.concatenate([zero, v, zero], axis=0)


def kernel(
    counts,
    old_hbm,
    init_hbm,
    shear_hbm,
    mobil_hbm,
    new_hbm,
    next_hbm,
    old,
    init,
    coef,
    coef_in,
    u,
    fu,
    start_in,
    primed,
    faces,
    node,
    halo,
    face_out,
    face_in,
    error,
    coarse_out,
    coarse_in,
    last_in,
    end_out,
    end_in,
    result,
    local_sem,
    write_sem,
    tm_send,
    tm_recv,
    coef_send,
    coef_recv,
    face_send,
    face_recv,
    coarse_send,
    coarse_recv,
):
    integral, widths = node_tables()
    table = [[integral[m][j] - (widths[m] if j == m else 0.0) for j in range(5)] for m in range(4)]
    slices, slabs = counts
    t, s = lax.axis_index("tm"), lax.axis_index("space")
    before, after = (lax.rem(t + slices - 1, slices), s), (lax.rem(t + 1, slices), s)
    below, above = (t, lax.rem(s + slabs - 1, slabs)), (t, lax.rem(s + 1, slabs))
    has_below, has_above, is_first = s > 0, s < slabs - 1, t == 0
    exists = (has_below, has_above)

    barrier = pltpu.get_barrier_semaphore()
    for device in (before, below, above):
        pl.semaphore_signal(barrier, inc=1, device_id=device, device_id_type=MESH)

    loads = [
        pltpu.make_async_copy(old_hbm.at[0], old, local_sem.at[0]),
        pltpu.make_async_copy(shear_hbm, coef.at[0, pl.ds(3, LAYERS)], local_sem.at[1]),
        pltpu.make_async_copy(mobil_hbm, coef.at[1, pl.ds(3, LAYERS)], local_sem.at[2]),
        pltpu.make_async_copy(init_hbm, init, local_sem.at[3]),
    ]
    for load in loads:
        load.start()
    for load in loads:
        load.wait()

    stiff, fluid = coef[0, 3 : 3 + LAYERS], coef[1, 3 : 3 + LAYERS]

    for m in range(4):
        for k in range(FIELD):
            total = table[m][0] * old[0, k]
            for j in range(1, 5):
                total = total + table[m][j] * old[j, k]
            u[m, k] = total
    for m in range(4):
        images = operator([padded(u[m, k]) for k in range(FIELD)], stiff, fluid, 0.25, 1)
        for k in range(FIELD):
            fu[m, k] = images[k]

    pl.semaphore_wait(barrier, 3)

    def remote(src, dst, send, recv, device):
        return pltpu.make_async_remote_copy(
            src_ref=src, dst_ref=dst, send_sem=send, recv_sem=recv, device_id=device, device_id_type=MESH
        )

    start_copy = remote(old.at[4], start_in, tm_send.at[0], tm_recv.at[0], after)
    start_copy.start()
    coef_copies = [
        remote(coef.at[:, pl.ds(3, 3)], coef_in.at[1], coef_send.at[0], coef_recv.at[1], below),
        remote(coef.at[:, pl.ds(6, 3)], coef_in.at[0], coef_send.at[1], coef_recv.at[0], above),
    ]
    for copy in coef_copies:
        copy.start()

    start_copy.wait_recv()
    for k in range(FIELD):
        first = jnp.where(is_first, init[k], start_in[k])
        node[0, k] = first
        primed[k] = padded(first)
    writes = [pltpu.make_async_copy(node.at[0], new_hbm.at[0, 0], write_sem.at[0])]
    writes[0].start()

    face_copies = []
    for m in range(5):
        for side, layer in ((0, 0), (1, LAYERS - 1)):
            for k in range(FIELD):
                face = primed[k, layer + 1]
                faces[side, m, k] = face
                if m < 4:
                    face_out[side, m, k] = widths[m] * face + u[m, k, layer]
        if m == 4:
            break
        for side, device in ((0, below), (1, above)):
            copy = remote(
                face_out.at[side, m],
                face_in.at[1 - side, m],
                face_send.at[side, m],
                face_recv.at[1 - side, m],
                device,
            )
            copy.start()
            face_copies.append(copy)
        images = operator([primed[k] for k in range(FIELD)], stiff, fluid, 0.25, 1)
        for k in range(FIELD):
            moved = primed[k, 1 : 1 + LAYERS] + widths[m] * images[k] + fu[m, k]
            primed[k, 1 : 1 + LAYERS] = moved
            if m == 0:
                node[1, k] = moved
                error[0, k] = images[k]

    for copy in coef_copies:
        copy.wait_recv()
    for array in range(2):
        coef[array, 0:3] = jnp.where(has_below, coef_in[0, array], 0.0)
        coef[array, 9:12] = jnp.where(has_above, coef_in[1, array], 0.0)
    gradients = [jnp.where(exists[side], 0.25, 0.0) for side in range(2)]

    def across(q, side):
        layer = (2, 9)[side]
        reach = (from_above, from_below)[side]
        return reach(q, coef[0, layer : layer + 1], coef[1, layer : layer + 1], gradients[side])

    for side in range(2):
        layer = (0, LAYERS - 1)[side]
        for m in range(4):
            z = []
            for k in range(FIELD):
                total = table[m][0] * faces[side, 0, k]
                for j in range(1, 5):
                    total = total + table[m][j] * faces[side, j, k]
                z.append((total - u[m, k, layer])[None])
            face_out[side, 4, m] = means(across(z, side))[0]
    for side, device in ((0, below), (1, above)):
        copy = remote(
            face_out.at[side, 4],
            face_in.at[1 - side, 4],
            face_send.at[side, 4],
            face_recv.at[1 - side, 4],
            device,
        )
        copy.start()
        face_copies.append(copy)

    def inflow(side, m):
        layer = (3, 8)[side]
        q = [jnp.where(exists[side], face_in[side, m, k], 0.0)[None] for k in range(FIELD)]
        reach = (from_below, from_above)[side]
        return reach(q, coef[0, layer : layer + 1], coef[1, layer : layer + 1], 0.25)

    def edge(m, side):
        return [u[m, k, (0, LAYERS - 1)[side]][None] for k in range(FIELD)]

    for side in range(2):
        face_copies[side].wait_recv()
    low, high = inflow(0, 0), inflow(1, 0)
    zero = jnp.zeros((2, 8, 128), jnp.float32)
    out_low = across([face_out[0, 0, k][None] for k in range(FIELD)], 0)
    out_high = across([face_out[1, 0, k][None] for k in range(FIELD)], 1)
    for k in range(FIELD):
        node[1, k] = ends(node[1, k], low[k], high[k])
        halo[0, k] = jnp.concatenate([zero, out_low[k]], axis=0)
        halo[1, k] = jnp.concatenate([out_high[k], zero], axis=0)

    sums = [means([layer_pairs(error[0, k]) for k in range(FIELD)])]
    grad = jnp.concatenate(
        [
            jnp.full((3, 8, 128), 1.0, jnp.float32) * gradients[0],
            jnp.full((LAYERS, 8, 128), 0.25, jnp.float32),
            jnp.full((3, 8, 128), 1.0, jnp.float32) * gradients[1],
        ],
        axis=0,
    )
    for m in range(1, 5):
        reach = (0, 2, 3, 1, 0)[m]
        own = slice(reach, reach + LAYERS)
        lo, hi = 3 - reach, 9 + reach
        q = []
        for k in range(FIELD):
            if reach == 3:
                whole = padded(jnp.concatenate([halo[0, k], node[m, k], halo[1, k]], axis=0))
            else:
                whole = jnp.concatenate(
                    [halo[0, k, 2 - reach :], node[m, k], halo[1, k, : reach + 1]], axis=0
                )
            q.append(whole)
        images = operator(q, coef[0, lo:hi], coef[1, lo:hi], grad[lo:hi], 1)
        sums.append(means([layer_pairs(images[k][own]) for k in range(FIELD)]))
        if m == 4:
            break
        for side in range(2):
            face_copies[2 * m + side].wait_recv()
        low, high = inflow(0, m), inflow(1, m)
        out_low, out_high = across(edge(m, 0), 0), across(edge(m, 1), 1)
        for k in range(FIELD):
            moved = node[m, k] + widths[m] * images[k][own] + fu[m, k]
            node[m + 1, k] = ends(moved, low[k], high[k])
            inner = halo[0, k, 3 - reach :] + widths[m] * images[k][:reach]
            halo[0, k, 3 - reach :] = jnp.concatenate([inner[:-1], inner[-1:] + out_low[k]], axis=0) if reach > 1 else inner + out_low[k]
            inner = halo[1, k, :reach] + widths[m] * images[k][reach + LAYERS :]
            halo[1, k, :reach] = jnp.concatenate([inner[:1] + out_high[k], inner[1:]], axis=0) if reach > 1 else inner + out_high[k]

    last_copy = remote(node.at[4], last_in, tm_send.at[1], tm_recv.at[1], after)
    last_copy.start()

    for side in range(2):
        face_copies[8 + side].wait_recv()
    for m in range(4):
        total = table[m][0] * sums[0]
        for j in range(1, 5):
            total = total + table[m][j] * sums[j]
        total = total - means([layer_pairs(fu[m, k]) for k in range(FIELD)])
        total = ends(
            total,
            jnp.where(has_below, face_in[0, 4, m], 0.0)[None],
            jnp.where(has_above, face_in[1, 4, m], 0.0)[None],
        )
        spread_out = spread(total)
        for k in range(FIELD):
            error[m, k, 0:3] = spread_out[k]

    def coarse_coef(lo, pairs):
        both = [
            jnp.concatenate([coef[a, lo + 2 * i : lo + 2 * i + 1] + coef[a, lo + 2 * i + 1 : lo + 2 * i + 2] for i in range(pairs)], axis=0)
            for a in range(2)
        ]
        pieces = spread(means([both[0], both[0], both[1], both[1]]))
        return 0.25 * pieces[0], 0.25 * pieces[2]

    coarse_stiff, coarse_fluid = coarse_coef(1, 5)
    weight = 0.5 * grad[2:10]
    coarse_grad = jnp.concatenate([weight[0:1], weight[1:4], weight[7:8]], axis=0)
    own_stiff, own_fluid = coarse_stiff[1:4], coarse_fluid[1:4]

    def send_coarse(m, d):
        for side, layer in ((0, 0), (1, 2)):
            coarse_out[side, m] = woven([d[k][layer : layer + 1] for k in range(FIELD)])[0]

    d1 = [error[0, k, 0:3] for k in range(FIELD)]
    send_coarse(0, d1)
    f1 = operator([padded(v) for v in d1], own_stiff, own_fluid, 0.125, 2)
    d2 = [d1[k] + widths[1] * f1[k] + error[1, k, 0:3] for k in range(FIELD)]
    send_coarse(1, d2)
    f2 = operator([padded(v) for v in d2], own_stiff, own_fluid, 0.125, 2)
    d3 = [d2[k] + widths[2] * f2[k] + error[2, k, 0:3] for k in range(FIELD)]
    send_coarse(2, d3)
    coarse_copies = []
    for side, device in ((0, below), (1, above)):
        copy = remote(
            coarse_out.at[side],
            coarse_in.at[1 - side],
            coarse_send.at[side],
            coarse_recv.at[1 - side],
            device,
        )
        copy.start()
        coarse_copies.append(copy)

    def finish(m, d):
        for k in range(FIELD):
            result[m - 1, k] = node[m, k] + twice(d[k])
        write = pltpu.make_async_copy(result.at[m - 1], new_hbm.at[0, m], write_sem.at[m])
        write.start()
        writes.append(write)

    finish(1, d1)

    def coarse_across(q, side):
        layer = (0, 4)[side]
        reach = (from_above, from_below)[side]
        part = slice(layer, layer + 1)
        return reach(q, coarse_stiff[part], coarse_fluid[part], coarse_grad[part])

    halo_low = [widths[1] * v for v in coarse_across([v[0:1] for v in d1], 0)]
    halo_high = [widths[1] * v for v in coarse_across([v[2:3] for v in d1], 1)]

    for copy in coarse_copies:
        copy.wait_recv()
    coming = [
        [spread(jnp.where(exists[side], coarse_in[side, m], 0.0)[None]) for m in range(3)] for side in range(2)
    ]

    def coarse_inflow(m):
        low = from_below(coming[0][m], own_stiff[0:1], own_fluid[0:1], 0.125)
        high = from_above(coming[1][m], own_stiff[2:3], own_fluid[2:3], 0.125)
        return low, high

    low, high = coarse_inflow(0)
    d2 = [ends(d2[k], widths[1] * low[k], widths[1] * high[k]) for k in range(FIELD)]
    finish(2, d2)
    low, high = coarse_inflow(1)
    q = [padded(jnp.concatenate([halo_low[k], d2[k], halo_high[k]], axis=0)) for k in range(FIELD)]
    images = operator(q, coarse_stiff, coarse_fluid, coarse_grad, 2)
    d3 = [
        d2[k] + widths[2] * ends(images[k][1:4], low[k], high[k]) + error[2, k, 0:3] for k in range(FIELD)
    ]
    finish(3, d3)
    halo_low = [halo_low[k] + widths[2] * images[k][0:1] + coming[0][2][k] for k in range(FIELD)]
    halo_high = [halo_high[k] + widths[2] * images[k][4:5] + coming[1][2][k] for k in range(FIELD)]
    q = [jnp.concatenate([halo_low[k], d3[k], halo_high[k]], axis=0) for k in range(FIELD)]
    images = operator(q, own_stiff, own_fluid, 0.125, 2)
    d4 = [d3[k] + widths[3] * images[k] + error[3, k, 0:3] for k in range(FIELD)]
    end_out[...] = woven(d4)
    end_copy = remote(end_out, end_in, tm_send.at[2], tm_recv.at[2], after)
    end_copy.start()
    finish(4, d4)

    last_copy.wait_recv()
    end_copy.wait_recv()
    d4 = spread(end_in[...])
    for k in range(FIELD):
        start_in[k] = jnp.where(is_first, init[k], last_in[k] + twice(d4[k]))
    write = pltpu.make_async_copy(start_in, next_hbm.at[0], write_sem.at[5])
    write.start()
    writes.append(write)

    for copy in [start_copy, last_copy, end_copy] + coef_copies + face_copies + coarse_copies:
        copy.wait_send()
    for write in writes:
        write.wait()


def on_device(counts, old_nodes, initial, shear_modulus, mobility):
    def vmem(*shape):
        return pltpu.VMEM(shape + (8, 128), jnp.float32)

    dma = pltpu.SemaphoreType.DMA
    return pl.pallas_call(
        functools.partial(kernel, counts),
        out_shape=(
            jax.ShapeDtypeStruct((1, 5, FIELD, LAYERS, 8, 128), jnp.float32),
            jax.ShapeDtypeStruct((1, FIELD, LAYERS, 8, 128), jnp.float32),
        ),
        in_specs=[pl.BlockSpec(memory_space=pl.ANY)] * 4,
        out_specs=(pl.BlockSpec(memory_space=pl.ANY),) * 2,
        scratch_shapes=[
            vmem(5, FIELD, LAYERS),
            vmem(FIELD, LAYERS),
            vmem(2, EXT),
            vmem(2, 2, 3),
            vmem(4, FIELD, LAYERS),
            vmem(4, FIELD, LAYERS),
            vmem(FIELD, LAYERS),
            vmem(FIELD, LAYERS + 2),
            vmem(2, 5, FIELD),
            vmem(5, FIELD, LAYERS),
            vmem(2, FIELD, 3),
            vmem(2, 5, FIELD),
            vmem(2, 5, FIELD),
            vmem(4, FIELD, LAYERS),
            vmem(2, 3),
            vmem(2, 3),
            vmem(FIELD, LAYERS),
            vmem(3),
            vmem(3),
            vmem(4, FIELD, LAYERS),
            dma((4,)),
            dma((6,)),
            dma((3,)),
            dma((3,)),
            dma((2,)),
            dma((2,)),
            dma((2, 5)),
            dma((2, 5)),
            dma((2,)),
            dma((2,)),
        ],
        compiler_params=pltpu.CompilerParams(
            collective_id=0, has_side_effects=True, vmem_limit_bytes=32 * 1024 * 1024
        ),
    )(old_nodes, initial, shear_modulus, mobility)


def solution(mesh):
    counts = (mesh.shape["tm"], mesh.shape["space"])
    return jax.shard_map(
        functools.partial(on_device, counts),
        mesh=mesh,
        in_specs=(
            P("tm", None, None, "space", None, None),
            P(None, "space", None, None),
            P("space", None, None),
            P("space", None, None),
        ),
        out_specs=(P("tm", None, None, "space", None, None), P("tm", None, "space", None, None)),
        check_vma=False,
    )
```

```python
import functools
import math

import jax
import jax.numpy as jnp
from jax import lax
from jax.experimental import pallas as pl
from jax.experimental.pallas import tpu as pltpu
from jax.sharding import PartitionSpec as P

MESH = pl.DeviceIdType.MESH
slice_step = 0.4
LAYERS = 6
EXT = 12
FIELD = 4


def node_tables():
    root_gap = math.sqrt(3.0 / 7.0)
    points = [0.0, (1.0 - root_gap) / 2.0, 0.5, (1.0 + root_gap) / 2.0, 1.0]
    polys = []
    for node in range(5):
        coeffs = [1.0]
        for other in range(5):
            if other != node:
                denom = points[node] - points[other]
                grown = [0.0] * (len(coeffs) + 1)
                for power in range(len(coeffs)):
                    grown[power + 1] += coeffs[power] / denom
                    grown[power] -= points[other] * coeffs[power] / denom
                coeffs = grown
        polys.append(coeffs)
    integral = []
    for column in range(4):
        lower = points[column]
        upper = points[column + 1]
        table_row = []
        for node in range(5):
            total = 0.0
            for power in range(5):
                total += (
                    polys[node][power] * (upper ** (power + 1) - lower ** (power + 1)) / (power + 1)
                )
            table_row.append(total * slice_step)
        integral.append(table_row)
    widths = [(points[column + 1] - points[column]) * slice_step for column in range(4)]
    return (integral, widths)


def positions(shape, axis):
    return lax.broadcasted_iota(jnp.int32, shape, axis)


def at(value, axis, step):
    size = value.shape[axis]
    moved = pltpu.roll(value, (-step) % size, axis)
    where = positions(value.shape, axis)
    inside = where < size - step if step > 0 else where >= -step
    return jnp.where(inside, moved, 0.0)


def operator(q, stiff, fluid, grad, step):
    out = [None] * 4
    diverge = None
    for k in (3, 0, 1, 2):
        center, below, above = q[k][1:-1], q[k][:-2], q[k][2:]
        xp, xm = at(center, 1, step), at(center, 1, -step)
        yp, ym = at(center, 2, step), at(center, 2, -step)
        laplace = ((xp + xm) + (yp + ym)) + (above + below) - 6.0 * center
        if k == 3:
            flow = fluid * laplace
            grads = [grad * (above - below), grad * (xp - xm), grad * (yp - ym)]
        else:
            out[k] = stiff * laplace - grads[k]
            part = (above - below, xp - xm, yp - ym)[k]
            diverge = part if diverge is None else diverge + part
    out[3] = flow - grad * diverge
    return out


def from_below(q, stiff, fluid, grad):
    return [stiff * q[0] + grad * q[3], stiff * q[1], stiff * q[2], fluid * q[3] + grad * q[0]]


def from_above(q, stiff, fluid, grad):
    return [stiff * q[0] - grad * q[3], stiff * q[1], stiff * q[2], fluid * q[3] - grad * q[0]]


def even(shape, axis):
    return positions(shape, axis) % 2 == 0


def pair_sums(a, b, axis):
    size = a.shape[axis]
    is_even = even(a.shape, axis)
    kept, other = jnp.where(is_even, a, b), jnp.where(is_even, b, a)
    return kept + jnp.where(is_even, pltpu.roll(other, size - 1, axis), pltpu.roll(other, 1, axis))


def means(q):
    return 0.125 * pair_sums(pair_sums(q[0], q[1], 2), pair_sums(q[2], q[3], 2), 1)


def layer_pairs(v):
    return jnp.concatenate([v[2 * i : 2 * i + 1] + v[2 * i + 1 : 2 * i + 2] for i in range(3)], axis=0)


def woven(q):
    shape = q[0].shape
    ye, xe = even(shape, 2), even(shape, 1)
    return jnp.where(xe, jnp.where(ye, q[0], q[1]), jnp.where(ye, q[2], q[3]))


def spread(p):
    ye, xe = even(p.shape, 2), even(p.shape, 1)
    a = jnp.where(ye, p, pltpu.roll(p, 1, 2))
    b = jnp.where(ye, pltpu.roll(p, 127, 2), p)
    return [
        jnp.where(xe, a, pltpu.roll(a, 1, 1)),
        jnp.where(xe, b, pltpu.roll(b, 1, 1)),
        jnp.where(xe, pltpu.roll(a, 7, 1), a),
        jnp.where(xe, pltpu.roll(b, 7, 1), b),
    ]


def twice(v):
    return jnp.concatenate([v[i // 2 : i // 2 + 1] for i in range(LAYERS)], axis=0)


def ends(v, low, high):
    return jnp.concatenate([v[:1] + low, v[1:-1], v[-1:] + high], axis=0)


def padded(v):
    zero = jnp.zeros_like(v[:1])
    return jnp.concatenate([zero, v, zero], axis=0)


def kernel(
    counts,
    old_hbm,
    init_hbm,
    shear_hbm,
    mobil_hbm,
    new_hbm,
    next_hbm,
    old,
    init,
    coef,
    coef_in,
    u,
    fu,
    start_in,
    primed,
    faces,
    node,
    halo,
    face_out,
    face_in,
    image,
    coarse_out,
    coarse_in,
    last_in,
    end_out,
    end_in,
    result,
    local_sem,
    write_sem,
    tm_send,
    tm_recv,
    coef_send,
    coef_recv,
    face_send,
    face_recv,
    coarse_send,
    coarse_recv,
    ready,
    later_ready,
):
    integral, widths = node_tables()
    table = [[integral[m][j] - (widths[m] if j == m else 0.0) for j in range(5)] for m in range(4)]
    slices, slabs = counts
    t, s = lax.axis_index("tm"), lax.axis_index("space")
    before, after = (lax.rem(t + slices - 1, slices), s), (lax.rem(t + 1, slices), s)
    below, above = (t, lax.rem(s + slabs - 1, slabs)), (t, lax.rem(s + 1, slabs))
    below_before, below_after = (before[0], below[1]), (after[0], below[1])
    above_before, above_after = (before[0], above[1]), (after[0], above[1])
    has_below, has_above, has_before, has_after = s > 0, s < slabs - 1, t > 0, t < slices - 1
    exists = (has_below, has_above)

    place = lax.rem(s, 4)
    greets = (
        jnp.logical_or(place == 0, place == 3),
        jnp.logical_or(place == 0, place == 1),
    )
    leads = tuple(jnp.logical_and(exists[side], greets[side]) for side in range(2))
    follows = tuple(jnp.logical_and(exists[side], jnp.logical_not(greets[side])) for side in range(2))
    barrier = pltpu.get_barrier_semaphore()
    for wanted, device in ((has_before, before), (leads[0], below), (leads[1], above)):

        @pl.when(wanted)
        def _():
            pl.semaphore_signal(barrier, inc=1, device_id=device, device_id_type=MESH)

    loads = [
        pltpu.make_async_copy(old_hbm.at[0], old, local_sem.at[0]),
        pltpu.make_async_copy(shear_hbm, coef.at[0, pl.ds(3, LAYERS)], local_sem.at[1]),
        pltpu.make_async_copy(mobil_hbm, coef.at[1, pl.ds(3, LAYERS)], local_sem.at[2]),
        pltpu.make_async_copy(init_hbm, init, local_sem.at[3]),
    ]
    for load in loads:
        load.start()
    for load in loads:
        load.wait()

    stiff, fluid = coef[0, 3 : 3 + LAYERS], coef[1, 3 : 3 + LAYERS]

    for m in range(4):
        for k in range(FIELD):
            total = table[m][0] * old[0, k]
            for j in range(1, 5):
                total = total + table[m][j] * old[j, k]
            u[m, k] = total
    for m in range(4):
        images = operator([padded(u[m, k]) for k in range(FIELD)], stiff, fluid, 0.25, 1)
        for k in range(FIELD):
            fu[m, k] = images[k]

    greeted = [jnp.where(c, 1, 0) for c in (has_after,) + follows]
    greeted = greeted[0] + greeted[1] + greeted[2]

    @pl.when(greeted > 0)
    def _():
        pl.semaphore_wait(barrier, greeted)

    def remote(src, dst, send, recv, device):
        return pltpu.make_async_remote_copy(
            src_ref=src, dst_ref=dst, send_sem=send, recv_sem=recv, device_id=device, device_id_type=MESH
        )

    def start_if(wanted, *copies):
        @pl.when(wanted)
        def _():
            for copy in copies:
                copy.start()

    def wait_if(wanted, *copies):
        @pl.when(wanted)
        def _():
            for copy in copies:
                copy.wait_recv()

    start_copy = remote(old.at[4], start_in, tm_send.at[0], tm_recv.at[0], after)
    start_if(has_after, start_copy)
    coef_copies = [
        remote(coef.at[:, pl.ds(3, 3)], coef_in.at[1], coef_send.at[0], coef_recv.at[1], below),
        remote(coef.at[:, pl.ds(6, 3)], coef_in.at[0], coef_send.at[1], coef_recv.at[0], above),
    ]
    for side, device in ((0, below), (1, above)):

        @pl.when(follows[side])
        def _():
            pl.semaphore_signal(ready.at[1 - side], inc=1, device_id=device, device_id_type=MESH)
            coef_copies[side].start()

        @pl.when(jnp.logical_not(exists[side]))
        def _():
            face_in[side] = jnp.zeros((5, FIELD, 8, 128), jnp.float32)
            coef_in[side] = jnp.zeros((2, 3, 8, 128), jnp.float32)
            coarse_in[:, side] = jnp.zeros((2, 3, 8, 128), jnp.float32)

    @pl.when(jnp.logical_not(has_before))
    def _():
        start_in[...] = init[...]

    wait_if(has_before, start_copy)
    for k in range(FIELD):
        first = start_in[k]
        node[0, k] = first
        primed[k] = padded(first)
    writes = [pltpu.make_async_copy(node.at[0], new_hbm.at[0, 0], write_sem.at[0])]
    writes[0].start()

    face_copies = []
    for m in range(5):
        for side, layer in ((0, 0), (1, LAYERS - 1)):
            for k in range(FIELD):
                face = primed[k, layer + 1]
                faces[side, m, k] = face
                if m < 4:
                    face_out[side, m, k] = widths[m] * face + u[m, k, layer]
        if m == 4:
            break
        for side, device in ((0, below), (1, above)):
            copy = remote(
                face_out.at[side, m],
                face_in.at[1 - side, m],
                face_send.at[side, m],
                face_recv.at[1 - side, m],
                device,
            )
            start_if(follows[side], copy)
            face_copies.append(copy)
        images = operator([primed[k] for k in range(FIELD)], stiff, fluid, 0.25, 1)
        for k in range(FIELD):
            moved = primed[k, 1 : 1 + LAYERS] + widths[m] * images[k] + fu[m, k]
            primed[k, 1 : 1 + LAYERS] = moved
            if m == 0:
                node[1, k] = moved
                image[k] = images[k]

    for side in (1, 0):

        @pl.when(leads[side])
        def _():
            pl.semaphore_wait(ready.at[side], 1)
            coef_copies[side].start()
            for m in range(4):
                face_copies[2 * m + side].start()

    for side in range(2):
        wait_if(exists[side], coef_copies[1 - side])
        for array in range(2):
            lo = (0, 9)[side]
            coef[array, lo : lo + 3] = coef_in[side, array]
    gradients = [jnp.where(exists[side], 0.25, 0.0) for side in range(2)]

    def across(q, side):
        layer = (2, 9)[side]
        reach = (from_above, from_below)[side]
        return reach(q, coef[0, layer : layer + 1], coef[1, layer : layer + 1], gradients[side])

    for side in range(2):
        layer = (0, LAYERS - 1)[side]
        for m in range(4):
            z = []
            for k in range(FIELD):
                total = table[m][0] * faces[side, 0, k]
                for j in range(1, 5):
                    total = total + table[m][j] * faces[side, j, k]
                z.append((total - u[m, k, layer])[None])
            face_out[side, 4, m] = means(across(z, side))[0]
    for side, device in ((0, below), (1, above)):
        copy = remote(
            face_out.at[side, 4],
            face_in.at[1 - side, 4],
            face_send.at[side, 4],
            face_recv.at[1 - side, 4],
            device,
        )
        start_if(exists[side], copy)
        face_copies.append(copy)

    def inflow(side, m):
        layer = (3, 8)[side]
        q = [face_in[side, m, k][None] for k in range(FIELD)]
        reach = (from_below, from_above)[side]
        return reach(q, coef[0, layer : layer + 1], coef[1, layer : layer + 1], 0.25)

    def edge(m, side):
        return [u[m, k, (0, LAYERS - 1)[side]][None] for k in range(FIELD)]

    for side, device in ((0, below_before), (1, above_before)):
        wait_if(exists[side], face_copies[1 - side])

        @pl.when(jnp.logical_and(exists[side], has_before))
        def _():
            pl.semaphore_signal(later_ready.at[1 - side], inc=1, device_id=device, device_id_type=MESH)

    low, high = inflow(0, 0), inflow(1, 0)
    zero = jnp.zeros((2, 8, 128), jnp.float32)
    out_low = across([face_out[0, 0, k][None] for k in range(FIELD)], 0)
    out_high = across([face_out[1, 0, k][None] for k in range(FIELD)], 1)
    for k in range(FIELD):
        node[1, k] = ends(node[1, k], low[k], high[k])
        halo[0, k] = jnp.concatenate([zero, out_low[k]], axis=0)
        halo[1, k] = jnp.concatenate([out_high[k], zero], axis=0)

    sums = [means([layer_pairs(image[k]) for k in range(FIELD)])]
    grad = jnp.concatenate(
        [
            jnp.full((3, 8, 128), 1.0, jnp.float32) * gradients[0],
            jnp.full((LAYERS, 8, 128), 0.25, jnp.float32),
            jnp.full((3, 8, 128), 1.0, jnp.float32) * gradients[1],
        ],
        axis=0,
    )
    for m in range(1, 5):
        reach = (0, 2, 3, 1, 0)[m]
        own = slice(reach, reach + LAYERS)
        lo, hi = 3 - reach, 9 + reach
        q = []
        for k in range(FIELD):
            if reach == 3:
                whole = padded(jnp.concatenate([halo[0, k], node[m, k], halo[1, k]], axis=0))
            else:
                whole = jnp.concatenate(
                    [halo[0, k, 2 - reach :], node[m, k], halo[1, k, : reach + 1]], axis=0
                )
            q.append(whole)
        images = operator(q, coef[0, lo:hi], coef[1, lo:hi], grad[lo:hi], 1)
        sums.append(means([layer_pairs(images[k][own]) for k in range(FIELD)]))
        if m == 4:
            break
        for side in range(2):
            wait_if(exists[side], face_copies[2 * m + 1 - side])
        low, high = inflow(0, m), inflow(1, m)
        out_low, out_high = across(edge(m, 0), 0), across(edge(m, 1), 1)
        for k in range(FIELD):
            moved = node[m, k] + widths[m] * images[k][own] + fu[m, k]
            node[m + 1, k] = ends(moved, low[k], high[k])
            inner = halo[0, k, 3 - reach :] + widths[m] * images[k][:reach]
            halo[0, k, 3 - reach :] = jnp.concatenate([inner[:-1], inner[-1:] + out_low[k]], axis=0) if reach > 1 else inner + out_low[k]
            inner = halo[1, k, :reach] + widths[m] * images[k][reach + LAYERS :]
            halo[1, k, :reach] = jnp.concatenate([inner[:1] + out_high[k], inner[1:]], axis=0) if reach > 1 else inner + out_high[k]

    for side in range(2):
        wait_if(exists[side], face_copies[9 - side])
    errors = []
    for m in range(4):
        total = table[m][0] * sums[0]
        for j in range(1, 5):
            total = total + table[m][j] * sums[j]
        total = total - means([layer_pairs(fu[m, k]) for k in range(FIELD)])
        total = ends(
            total,
            face_in[0, 4, m][None],
            face_in[1, 4, m][None],
        )
        end_out[m] = total
        errors.append(spread(total))

    def coarse_coef(lo, pairs):
        both = [
            jnp.concatenate(
                [
                    coef[a, lo + 2 * i : lo + 2 * i + 1] + coef[a, lo + 2 * i + 1 : lo + 2 * i + 2]
                    for i in range(pairs)
                ],
                axis=0,
            )
            for a in range(2)
        ]
        pieces = spread(means([both[0], both[0], both[1], both[1]]))
        return 0.25 * pieces[0], 0.25 * pieces[2]

    coarse_stiff, coarse_fluid = coarse_coef(1, 5)
    weight = 0.5 * grad[2:10]
    coarse_grad = jnp.concatenate([weight[0:1], weight[1:4], weight[7:8]], axis=0)
    own_stiff, own_fluid = coarse_stiff[1:4], coarse_fluid[1:4]

    def sweep_alone(e):
        d = [[e[0][k] for k in range(FIELD)]]
        for m in (1, 2):
            images = operator([padded(v) for v in d[-1]], own_stiff, own_fluid, 0.125, 2)
            d.append([d[-1][k] + widths[m] * images[k] + e[m][k] for k in range(FIELD)])
        return d

    alone = sweep_alone(errors)
    for m in range(3):
        for side, layer in ((0, 0), (1, 2)):
            coarse_out[side, m] = woven([alone[m][k][layer : layer + 1] for k in range(FIELD)])[0]
    end_copies = [remote(end_out, end_in, tm_send.at[2], tm_recv.at[2], after)]
    coarse_copies = []
    for side, device, later in ((0, below, below_after), (1, above, above_after)):
        coarse_copies.append(
            remote(
                coarse_out.at[side],
                coarse_in.at[0, 1 - side],
                coarse_send.at[0, side],
                coarse_recv.at[0, 1 - side],
                device,
            )
        )
        end_copies.append(
            remote(
                coarse_out.at[side],
                coarse_in.at[1, 1 - side],
                coarse_send.at[1, side],
                coarse_recv.at[1, 1 - side],
                later,
            )
        )
    for side in range(2):
        start_if(exists[side], coarse_copies[side])
    last_copy = remote(node.at[4], last_in, tm_send.at[1], tm_recv.at[1], after)
    start_if(has_after, end_copies[0], last_copy)
    for side in range(2):

        @pl.when(jnp.logical_and(exists[side], has_after))
        def _():
            pl.semaphore_wait(later_ready.at[side], 1)
            end_copies[1 + side].start()

    def finish(m, d):
        for k in range(FIELD):
            result[m - 1, k] = node[m, k] + twice(d[k])
        write = pltpu.make_async_copy(result.at[m - 1], new_hbm.at[0, m], write_sem.at[m])
        write.start()
        writes.append(write)

    finish(1, alone[0])

    def coarse_across(q, side):
        layer = (0, 4)[side]
        reach = (from_above, from_below)[side]
        part = slice(layer, layer + 1)
        return reach(q, coarse_stiff[part], coarse_fluid[part], coarse_grad[part])

    def sweep(e, d, slot, arrivals):
        d1, d2 = d[0], d[1]
        halo_low = [widths[1] * v for v in coarse_across([v[0:1] for v in d1], 0)]
        halo_high = [widths[1] * v for v in coarse_across([v[2:3] for v in d1], 1)]
        for side in range(2):
            wait_if(exists[side], arrivals[1 - side])
        coming = [
            [spread(coarse_in[slot, side, m][None]) for m in range(3)]
            for side in range(2)
        ]

        def coarse_inflow(m):
            low = from_below(coming[0][m], own_stiff[0:1], own_fluid[0:1], 0.125)
            high = from_above(coming[1][m], own_stiff[2:3], own_fluid[2:3], 0.125)
            return low, high

        low, high = coarse_inflow(0)
        d2 = [ends(d2[k], widths[1] * low[k], widths[1] * high[k]) for k in range(FIELD)]
        low, high = coarse_inflow(1)
        q = [padded(jnp.concatenate([halo_low[k], d2[k], halo_high[k]], axis=0)) for k in range(FIELD)]
        images = operator(q, coarse_stiff, coarse_fluid, coarse_grad, 2)
        d3 = [
            d2[k] + widths[2] * ends(images[k][1:4], low[k], high[k]) + e[2][k] for k in range(FIELD)
        ]
        halo_low = [halo_low[k] + widths[2] * images[k][0:1] for k in range(FIELD)]
        halo_high = [halo_high[k] + widths[2] * images[k][4:5] for k in range(FIELD)]
        halo_low = [halo_low[k] + coming[0][2][k] for k in range(FIELD)]
        halo_high = [halo_high[k] + coming[1][2][k] for k in range(FIELD)]
        q = [jnp.concatenate([halo_low[k], d3[k], halo_high[k]], axis=0) for k in range(FIELD)]
        images = operator(q, own_stiff, own_fluid, 0.125, 2)
        d4 = [d3[k] + widths[3] * images[k] + e[3][k] for k in range(FIELD)]
        return d2, d3, d4

    d2, d3, d4 = sweep(errors, alone, 0, coarse_copies)
    finish(2, d2)
    finish(3, d3)
    finish(4, d4)

    @pl.when(has_before)
    def _():
        end_copies[0].wait_recv()
        errors = [spread(end_in[m]) for m in range(4)]
        d4 = sweep(errors, sweep_alone(errors), 1, end_copies[1:])[2]
        last_copy.wait_recv()
        for k in range(FIELD):
            start_in[k] = last_in[k] + twice(d4[k])

    write = pltpu.make_async_copy(start_in, next_hbm.at[0], write_sem.at[5])
    write.start()
    writes.append(write)

    def sent_if(wanted, *copies):
        @pl.when(wanted)
        def _():
            for copy in copies:
                copy.wait_send()

    sent_if(has_after, start_copy, last_copy, end_copies[0])
    for side in range(2):
        sent_if(exists[side], coef_copies[side], coarse_copies[side], *face_copies[side::2])
        sent_if(jnp.logical_and(exists[side], has_after), end_copies[1 + side])
    for write in writes:
        write.wait()


def on_device(counts, old_nodes, initial, shear_modulus, mobility):
    def vmem(*shape):
        return pltpu.VMEM(shape + (8, 128), jnp.float32)

    dma = pltpu.SemaphoreType.DMA
    return pl.pallas_call(
        functools.partial(kernel, counts),
        out_shape=(
            jax.ShapeDtypeStruct((1, 5, FIELD, LAYERS, 8, 128), jnp.float32),
            jax.ShapeDtypeStruct((1, FIELD, LAYERS, 8, 128), jnp.float32),
        ),
        in_specs=[pl.BlockSpec(memory_space=pltpu.HBM)] * 4,
        out_specs=(pl.BlockSpec(memory_space=pl.ANY),) * 2,
        scratch_shapes=[
            vmem(5, FIELD, LAYERS),
            vmem(FIELD, LAYERS),
            vmem(2, EXT),
            vmem(2, 2, 3),
            vmem(4, FIELD, LAYERS),
            vmem(4, FIELD, LAYERS),
            vmem(FIELD, LAYERS),
            vmem(FIELD, LAYERS + 2),
            vmem(2, 5, FIELD),
            vmem(5, FIELD, LAYERS),
            vmem(2, FIELD, 3),
            vmem(2, 5, FIELD),
            vmem(2, 5, FIELD),
            vmem(FIELD, LAYERS),
            vmem(2, 3),
            vmem(2, 2, 3),
            vmem(FIELD, LAYERS),
            vmem(4, 3),
            vmem(4, 3),
            vmem(4, FIELD, LAYERS),
            dma((4,)),
            dma((6,)),
            dma((3,)),
            dma((3,)),
            dma((2,)),
            dma((2,)),
            dma((2, 5)),
            dma((2, 5)),
            dma((2, 2)),
            dma((2, 2)),
            pltpu.SemaphoreType.REGULAR((2,)),
            pltpu.SemaphoreType.REGULAR((2,)),
        ],
        compiler_params=pltpu.CompilerParams(
            collective_id=0, has_side_effects=True, vmem_limit_bytes=63 * 1024 * 1024
        ),
    )(old_nodes, initial, shear_modulus, mobility)


def solution(mesh):
    counts = (mesh.shape["tm"], mesh.shape["space"])
    return jax.shard_map(
        functools.partial(on_device, counts),
        mesh=mesh,
        in_specs=(
            P("tm", None, None, "space", None, None),
            P(None, "space", None, None),
            P("space", None, None),
            P("space", None, None),
        ),
        out_specs=(P("tm", None, None, "space", None, None), P("tm", None, "space", None, None)),
        check_vma=False,
    )
```

```python
import functools
import math

import jax
import jax.numpy as jnp
from jax import lax
from jax.experimental import pallas as pl
from jax.experimental.pallas import tpu as pltpu
from jax.sharding import PartitionSpec as P

MESH = pl.DeviceIdType.MESH
slice_step = 0.4
LAYERS = 6
EXT = 12
FIELD = 4


def node_tables():
    root_gap = math.sqrt(3.0 / 7.0)
    points = [0.0, (1.0 - root_gap) / 2.0, 0.5, (1.0 + root_gap) / 2.0, 1.0]
    polys = []
    for node in range(5):
        coeffs = [1.0]
        for other in range(5):
            if other != node:
                denom = points[node] - points[other]
                grown = [0.0] * (len(coeffs) + 1)
                for power in range(len(coeffs)):
                    grown[power + 1] += coeffs[power] / denom
                    grown[power] -= points[other] * coeffs[power] / denom
                coeffs = grown
        polys.append(coeffs)
    integral = []
    for column in range(4):
        lower = points[column]
        upper = points[column + 1]
        table_row = []
        for node in range(5):
            total = 0.0
            for power in range(5):
                total += (
                    polys[node][power] * (upper ** (power + 1) - lower ** (power + 1)) / (power + 1)
                )
            table_row.append(total * slice_step)
        integral.append(table_row)
    widths = [(points[column + 1] - points[column]) * slice_step for column in range(4)]
    return (integral, widths)


def positions(shape, axis):
    return lax.broadcasted_iota(jnp.int32, shape, axis)


def at(value, axis, step):
    size = value.shape[axis]
    moved = pltpu.roll(value, (-step) % size, axis)
    where = positions(value.shape, axis)
    inside = where < size - step if step > 0 else where >= -step
    return jnp.where(inside, moved, 0.0)


def operator(q, stiff, fluid, grad, step):
    out = [None] * 4
    diverge = None
    for k in (3, 0, 1, 2):
        center, below, above = q[k][1:-1], q[k][:-2], q[k][2:]
        xp, xm = at(center, 1, step), at(center, 1, -step)
        yp, ym = at(center, 2, step), at(center, 2, -step)
        laplace = ((xp + xm) + (yp + ym)) + (above + below) - 6.0 * center
        if k == 3:
            flow = fluid * laplace
            grads = [grad * (above - below), grad * (xp - xm), grad * (yp - ym)]
        else:
            out[k] = stiff * laplace - grads[k]
            part = (above - below, xp - xm, yp - ym)[k]
            diverge = part if diverge is None else diverge + part
    out[3] = flow - grad * diverge
    return out


def from_below(q, stiff, fluid, grad):
    return [stiff * q[0] + grad * q[3], stiff * q[1], stiff * q[2], fluid * q[3] + grad * q[0]]


def from_above(q, stiff, fluid, grad):
    return [stiff * q[0] - grad * q[3], stiff * q[1], stiff * q[2], fluid * q[3] - grad * q[0]]


def even(shape, axis):
    return positions(shape, axis) % 2 == 0


def pair_sums(a, b, axis):
    size = a.shape[axis]
    is_even = even(a.shape, axis)
    kept, other = jnp.where(is_even, a, b), jnp.where(is_even, b, a)
    return kept + jnp.where(is_even, pltpu.roll(other, size - 1, axis), pltpu.roll(other, 1, axis))


def means(q):
    return 0.125 * pair_sums(pair_sums(q[0], q[1], 2), pair_sums(q[2], q[3], 2), 1)


def layer_pairs(v):
    return jnp.concatenate([v[2 * i : 2 * i + 1] + v[2 * i + 1 : 2 * i + 2] for i in range(3)], axis=0)


def woven(q):
    shape = q[0].shape
    ye, xe = even(shape, 2), even(shape, 1)
    return jnp.where(xe, jnp.where(ye, q[0], q[1]), jnp.where(ye, q[2], q[3]))


def spread(p):
    ye, xe = even(p.shape, 2), even(p.shape, 1)
    a = jnp.where(ye, p, pltpu.roll(p, 1, 2))
    b = jnp.where(ye, pltpu.roll(p, 127, 2), p)
    return [
        jnp.where(xe, a, pltpu.roll(a, 1, 1)),
        jnp.where(xe, b, pltpu.roll(b, 1, 1)),
        jnp.where(xe, pltpu.roll(a, 7, 1), a),
        jnp.where(xe, pltpu.roll(b, 7, 1), b),
    ]


def twice(v):
    return jnp.concatenate([v[i // 2 : i // 2 + 1] for i in range(LAYERS)], axis=0)


def ends(v, low, high):
    return jnp.concatenate([v[:1] + low, v[1:-1], v[-1:] + high], axis=0)


def padded(v):
    zero = jnp.zeros_like(v[:1])
    return jnp.concatenate([zero, v, zero], axis=0)


def kernel(
    counts,
    old_hbm,
    rest_hbm,
    new_hbm,
    next_hbm,
    old,
    init,
    coef,
    coef_in,
    u,
    fu,
    start_in,
    primed,
    faces,
    node,
    halo,
    face_out,
    face_in,
    image,
    coarse_out,
    coarse_in,
    last_in,
    end_out,
    end_in,
    result,
    local_sem,
    write_sem,
    tm_send,
    tm_recv,
    coef_send,
    coef_recv,
    face_send,
    face_recv,
    coarse_send,
    coarse_recv,
    ready,
    later_ready,
):
    integral, widths = node_tables()
    table = [[integral[m][j] - (widths[m] if j == m else 0.0) for j in range(5)] for m in range(4)]
    slices, slabs = counts
    t, s = lax.axis_index("tm"), lax.axis_index("space")
    before, after = (lax.rem(t + slices - 1, slices), s), (lax.rem(t + 1, slices), s)
    below, above = (t, lax.rem(s + slabs - 1, slabs)), (t, lax.rem(s + 1, slabs))
    below_after, above_after = (after[0], below[1]), (after[0], above[1])
    has_below, has_above, has_before, has_after = s > 0, s < slabs - 1, t > 0, t < slices - 1
    exists = (has_below, has_above)

    place = lax.rem(s, 4)
    greets = (
        jnp.logical_or(place == 0, place == 3),
        jnp.logical_or(place == 0, place == 1),
    )
    leads = tuple(jnp.logical_and(exists[side], greets[side]) for side in range(2))
    follows = tuple(jnp.logical_and(exists[side], jnp.logical_not(greets[side])) for side in range(2))
    barrier = pltpu.get_barrier_semaphore()
    for wanted, device in ((has_before, before), (leads[0], below), (leads[1], above)):

        @pl.when(wanted)
        def _():
            pl.semaphore_signal(barrier, inc=1, device_id=device, device_id_type=MESH)

    loads = [
        pltpu.make_async_copy(old_hbm.at[0], old, local_sem.at[0]),
        pltpu.make_async_copy(rest_hbm.at[FIELD], coef.at[0, pl.ds(3, LAYERS)], local_sem.at[1]),
        pltpu.make_async_copy(rest_hbm.at[FIELD + 1], coef.at[1, pl.ds(3, LAYERS)], local_sem.at[2]),
        pltpu.make_async_copy(rest_hbm.at[pl.ds(0, FIELD)], init, local_sem.at[3]),
    ]
    for load in loads:
        load.start()
    for load in loads:
        load.wait()

    stiff, fluid = coef[0, 3 : 3 + LAYERS], coef[1, 3 : 3 + LAYERS]

    for m in range(4):
        for k in range(FIELD):
            total = table[m][0] * old[0, k]
            for j in range(1, 5):
                total = total + table[m][j] * old[j, k]
            u[m, k] = total
    for m in range(4):
        images = operator([padded(u[m, k]) for k in range(FIELD)], stiff, fluid, 0.25, 1)
        for k in range(FIELD):
            fu[m, k] = images[k]

    greeted = [jnp.where(c, 1, 0) for c in (has_after,) + follows]
    greeted = greeted[0] + greeted[1] + greeted[2]

    @pl.when(greeted > 0)
    def _():
        pl.semaphore_wait(barrier, greeted)

    def remote(src, dst, send, recv, device):
        return pltpu.make_async_remote_copy(
            src_ref=src, dst_ref=dst, send_sem=send, recv_sem=recv, device_id=device, device_id_type=MESH
        )

    def start_if(wanted, *copies):
        @pl.when(wanted)
        def _():
            for copy in copies:
                copy.start()

    def wait_if(wanted, *copies):
        @pl.when(wanted)
        def _():
            for copy in copies:
                copy.wait_recv()

    start_copy = remote(old.at[4], start_in, tm_send.at[0], tm_recv.at[0], after)
    start_if(has_after, start_copy)
    coef_copies = [
        remote(coef.at[:, pl.ds(3, 1)], coef_in.at[1, :, pl.ds(0, 1)], coef_send.at[0, 0], coef_recv.at[0, 1], below),
        remote(coef.at[:, pl.ds(8, 1)], coef_in.at[0, :, pl.ds(2, 1)], coef_send.at[0, 1], coef_recv.at[0, 0], above),
    ]
    deep_copies = [
        remote(coef.at[:, pl.ds(4, 1)], coef_in.at[1, :, pl.ds(1, 1)], coef_send.at[1, 0], coef_recv.at[1, 1], below),
        remote(coef.at[:, pl.ds(7, 1)], coef_in.at[0, :, pl.ds(1, 1)], coef_send.at[1, 1], coef_recv.at[1, 0], above),
    ]
    for side, device in ((0, below), (1, above)):

        @pl.when(follows[side])
        def _():
            pl.semaphore_signal(ready.at[1 - side], inc=1, device_id=device, device_id_type=MESH)
            coef_copies[side].start()
            deep_copies[side].start()

        @pl.when(jnp.logical_not(exists[side]))
        def _():
            face_in[side] = jnp.zeros((5, FIELD, 8, 128), jnp.float32)
            coef_in[side] = jnp.zeros((2, 3, 8, 128), jnp.float32)
            coarse_in[:, side] = jnp.zeros((2, 3, 8, 128), jnp.float32)

    @pl.when(jnp.logical_not(has_before))
    def _():
        start_in[...] = init[...]

    wait_if(has_before, start_copy)

    def pass_on(side):
        @pl.when(has_before)
        def _():
            pl.semaphore_signal(later_ready.at[side], inc=1, device_id=before, device_id_type=MESH)

    for side in range(2):

        @pl.when(follows[side])
        def _():
            pass_on(side)

    for k in range(FIELD):
        first = start_in[k]
        node[0, k] = first
        primed[k] = padded(first)
    writes = [pltpu.make_async_copy(node.at[0], new_hbm.at[0, 0], write_sem.at[0])]
    writes[0].start()

    face_copies = []
    for m in range(5):
        for side, layer in ((0, 0), (1, LAYERS - 1)):
            for k in range(FIELD):
                face = primed[k, layer + 1]
                faces[side, m, k] = face
                if m < 4:
                    face_out[side, m, k] = widths[m] * face + u[m, k, layer]
        if m == 4:
            break
        for side, device in ((0, below), (1, above)):
            copy = remote(
                face_out.at[side, m],
                face_in.at[1 - side, m],
                face_send.at[side, m],
                face_recv.at[1 - side, m],
                device,
            )
            start_if(follows[side], copy)
            face_copies.append(copy)
        images = operator([primed[k] for k in range(FIELD)], stiff, fluid, 0.25, 1)
        for k in range(FIELD):
            moved = primed[k, 1 : 1 + LAYERS] + widths[m] * images[k] + fu[m, k]
            primed[k, 1 : 1 + LAYERS] = moved
            if m == 0:
                node[1, k] = moved
                image[k] = images[k]

    for side in (1, 0):

        @pl.when(leads[side])
        def _():
            pl.semaphore_wait(ready.at[side], 1)
            coef_copies[side].start()
            face_copies[side].start()
            pass_on(side)
            face_copies[2 + side].start()
            deep_copies[side].start()
            face_copies[4 + side].start()
            face_copies[6 + side].start()

    for side in range(2):
        wait_if(exists[side], coef_copies[1 - side])
        for array in range(2):
            lo, layer = ((2, 2), (9, 0))[side]
            coef[array, lo : lo + 1] = coef_in[side, array, layer : layer + 1]
    gradients = [jnp.where(exists[side], 0.25, 0.0) for side in range(2)]

    def across(q, side):
        layer = (2, 9)[side]
        reach = (from_above, from_below)[side]
        return reach(q, coef[0, layer : layer + 1], coef[1, layer : layer + 1], gradients[side])

    for side in range(2):
        layer = (0, LAYERS - 1)[side]
        for m in range(4):
            z = []
            for k in range(FIELD):
                total = table[m][0] * faces[side, 0, k]
                for j in range(1, 5):
                    total = total + table[m][j] * faces[side, j, k]
                z.append((total - u[m, k, layer])[None])
            face_out[side, 4, m] = means(across(z, side))[0]
    for side, device in ((0, below), (1, above)):
        copy = remote(
            face_out.at[side, 4],
            face_in.at[1 - side, 4],
            face_send.at[side, 4],
            face_recv.at[1 - side, 4],
            device,
        )
        start_if(exists[side], copy)
        face_copies.append(copy)

    def inflow(side, m):
        layer = (3, 8)[side]
        q = [face_in[side, m, k][None] for k in range(FIELD)]
        reach = (from_below, from_above)[side]
        return reach(q, coef[0, layer : layer + 1], coef[1, layer : layer + 1], 0.25)

    def edge(m, side):
        return [u[m, k, (0, LAYERS - 1)[side]][None] for k in range(FIELD)]

    for side in range(2):
        wait_if(exists[side], face_copies[1 - side])
    low, high = inflow(0, 0), inflow(1, 0)
    zero = jnp.zeros((2, 8, 128), jnp.float32)
    out_low = across([face_out[0, 0, k][None] for k in range(FIELD)], 0)
    out_high = across([face_out[1, 0, k][None] for k in range(FIELD)], 1)
    for k in range(FIELD):
        node[1, k] = ends(node[1, k], low[k], high[k])
        halo[0, k] = jnp.concatenate([zero, out_low[k]], axis=0)
        halo[1, k] = jnp.concatenate([out_high[k], zero], axis=0)

    sums = [means([layer_pairs(image[k]) for k in range(FIELD)])]
    grad = jnp.concatenate(
        [
            jnp.full((3, 8, 128), 1.0, jnp.float32) * gradients[0],
            jnp.full((LAYERS, 8, 128), 0.25, jnp.float32),
            jnp.full((3, 8, 128), 1.0, jnp.float32) * gradients[1],
        ],
        axis=0,
    )
    for m in range(1, 5):
        if m == 1:
            for side in range(2):
                wait_if(exists[side], deep_copies[1 - side])
                for array in range(2):
                    lo = (1, 10)[side]
                    coef[array, lo : lo + 1] = coef_in[side, array, 1:2]
        reach = (0, 2, 2, 1, 0)[m]
        own = slice(reach, reach + LAYERS)
        lo, hi = 3 - reach, 9 + reach
        q = []
        for k in range(FIELD):
            q.append(
                jnp.concatenate([halo[0, k, 2 - reach :], node[m, k], halo[1, k, : reach + 1]], axis=0)
            )
        images = operator(q, coef[0, lo:hi], coef[1, lo:hi], grad[lo:hi], 1)
        sums.append(means([layer_pairs(images[k][own]) for k in range(FIELD)]))
        if m == 4:
            break
        for side in range(2):
            wait_if(exists[side], face_copies[2 * m + 1 - side])
        low, high = inflow(0, m), inflow(1, m)
        out_low, out_high = across(edge(m, 0), 0), across(edge(m, 1), 1)
        for k in range(FIELD):
            moved = node[m, k] + widths[m] * images[k][own] + fu[m, k]
            node[m + 1, k] = ends(moved, low[k], high[k])
            inner = halo[0, k, 3 - reach :] + widths[m] * images[k][:reach]
            halo[0, k, 3 - reach :] = jnp.concatenate([inner[:-1], inner[-1:] + out_low[k]], axis=0) if reach > 1 else inner + out_low[k]
            inner = halo[1, k, :reach] + widths[m] * images[k][reach + LAYERS :]
            halo[1, k, :reach] = jnp.concatenate([inner[:1] + out_high[k], inner[1:]], axis=0) if reach > 1 else inner + out_high[k]

    for side in range(2):
        wait_if(exists[side], face_copies[9 - side])
    errors = []
    for m in range(4):
        total = table[m][0] * sums[0]
        for j in range(1, 5):
            total = total + table[m][j] * sums[j]
        total = total - means([layer_pairs(fu[m, k]) for k in range(FIELD)])
        total = ends(
            total,
            face_in[0, 4, m][None],
            face_in[1, 4, m][None],
        )
        end_out[m] = total
        errors.append(spread(total))

    def coarse_coef(lo, pairs):
        both = [
            jnp.concatenate(
                [
                    coef[a, lo + 2 * i : lo + 2 * i + 1] + coef[a, lo + 2 * i + 1 : lo + 2 * i + 2]
                    for i in range(pairs)
                ],
                axis=0,
            )
            for a in range(2)
        ]
        pieces = spread(means([both[0], both[0], both[1], both[1]]))
        return 0.25 * pieces[0], 0.25 * pieces[2]

    coarse_stiff, coarse_fluid = coarse_coef(1, 5)
    weight = 0.5 * grad[2:10]
    coarse_grad = jnp.concatenate([weight[0:1], weight[1:4], weight[7:8]], axis=0)
    own_stiff, own_fluid = coarse_stiff[1:4], coarse_fluid[1:4]

    def sweep_alone(e):
        d = [[e[0][k] for k in range(FIELD)]]
        for m in (1, 2):
            images = operator([padded(v) for v in d[-1]], own_stiff, own_fluid, 0.125, 2)
            d.append([d[-1][k] + widths[m] * images[k] + e[m][k] for k in range(FIELD)])
        return d

    alone = sweep_alone(errors)
    for m in range(3):
        for side, layer in ((0, 0), (1, 2)):
            coarse_out[side, m] = woven([alone[m][k][layer : layer + 1] for k in range(FIELD)])[0]
    end_copies = [remote(end_out, end_in, tm_send.at[2], tm_recv.at[2], after)]
    coarse_copies = []
    for side, device, later in ((0, below, below_after), (1, above, above_after)):
        coarse_copies.append(
            remote(
                coarse_out.at[side],
                coarse_in.at[0, 1 - side],
                coarse_send.at[0, side],
                coarse_recv.at[0, 1 - side],
                device,
            )
        )
        end_copies.append(
            remote(
                coarse_out.at[side],
                coarse_in.at[1, 1 - side],
                coarse_send.at[1, side],
                coarse_recv.at[1, 1 - side],
                later,
            )
        )
    for side in range(2):
        start_if(exists[side], coarse_copies[side])
    last_copy = remote(node.at[4], last_in, tm_send.at[1], tm_recv.at[1], after)
    start_if(has_after, end_copies[0], last_copy)
    for side in range(2):

        @pl.when(jnp.logical_and(exists[side], has_after))
        def _():
            pl.semaphore_wait(later_ready.at[side], 1)
            end_copies[1 + side].start()

    def finish(m, d):
        for k in range(FIELD):
            result[m - 1, k] = node[m, k] + twice(d[k])
        write = pltpu.make_async_copy(result.at[m - 1], new_hbm.at[0, m], write_sem.at[m])
        write.start()
        writes.append(write)

    finish(1, alone[0])

    def coarse_across(q, side):
        layer = (0, 4)[side]
        reach = (from_above, from_below)[side]
        part = slice(layer, layer + 1)
        return reach(q, coarse_stiff[part], coarse_fluid[part], coarse_grad[part])

    def sweep(e, d, slot, arrivals):
        d1, d2 = d[0], d[1]
        halo_low = [widths[1] * v for v in coarse_across([v[0:1] for v in d1], 0)]
        halo_high = [widths[1] * v for v in coarse_across([v[2:3] for v in d1], 1)]
        for side in range(2):
            wait_if(exists[side], arrivals[1 - side])
        coming = [
            [spread(coarse_in[slot, side, m][None]) for m in range(3)]
            for side in range(2)
        ]

        def coarse_inflow(m):
            low = from_below(coming[0][m], own_stiff[0:1], own_fluid[0:1], 0.125)
            high = from_above(coming[1][m], own_stiff[2:3], own_fluid[2:3], 0.125)
            return low, high

        low, high = coarse_inflow(0)
        d2 = [ends(d2[k], widths[1] * low[k], widths[1] * high[k]) for k in range(FIELD)]
        low, high = coarse_inflow(1)
        q = [padded(jnp.concatenate([halo_low[k], d2[k], halo_high[k]], axis=0)) for k in range(FIELD)]
        images = operator(q, coarse_stiff, coarse_fluid, coarse_grad, 2)
        d3 = [
            d2[k] + widths[2] * ends(images[k][1:4], low[k], high[k]) + e[2][k] for k in range(FIELD)
        ]
        halo_low = [halo_low[k] + widths[2] * images[k][0:1] for k in range(FIELD)]
        halo_high = [halo_high[k] + widths[2] * images[k][4:5] for k in range(FIELD)]
        halo_low = [halo_low[k] + coming[0][2][k] for k in range(FIELD)]
        halo_high = [halo_high[k] + coming[1][2][k] for k in range(FIELD)]
        q = [jnp.concatenate([halo_low[k], d3[k], halo_high[k]], axis=0) for k in range(FIELD)]
        images = operator(q, own_stiff, own_fluid, 0.125, 2)
        d4 = [d3[k] + widths[3] * images[k] + e[3][k] for k in range(FIELD)]
        return d2, d3, d4

    d2, d3, d4 = sweep(errors, alone, 0, coarse_copies)
    finish(2, d2)
    finish(3, d3)
    finish(4, d4)

    @pl.when(has_before)
    def _():
        end_copies[0].wait_recv()
        errors = [spread(end_in[m]) for m in range(4)]
        d4 = sweep(errors, sweep_alone(errors), 1, end_copies[1:])[2]
        last_copy.wait_recv()
        for k in range(FIELD):
            start_in[k] = last_in[k] + twice(d4[k])

    write = pltpu.make_async_copy(start_in, next_hbm.at[0], write_sem.at[5])
    write.start()
    writes.append(write)

    def sent_if(wanted, *copies):
        @pl.when(wanted)
        def _():
            for copy in copies:
                copy.wait_send()

    sent_if(has_after, start_copy, last_copy, end_copies[0])
    for side in range(2):
        sent_if(exists[side], coef_copies[side], deep_copies[side], coarse_copies[side], *face_copies[side::2])
        sent_if(jnp.logical_and(exists[side], has_after), end_copies[1 + side])
    for write in writes:
        write.wait()


def on_device(counts, old_nodes, initial, shear_modulus, mobility):
    def vmem(*shape):
        return pltpu.VMEM(shape + (8, 128), jnp.float32)

    dma = pltpu.SemaphoreType.DMA
    return pl.pallas_call(
        functools.partial(kernel, counts),
        out_shape=(
            jax.ShapeDtypeStruct((1, 5, FIELD, LAYERS, 8, 128), jnp.float32),
            jax.ShapeDtypeStruct((1, FIELD, LAYERS, 8, 128), jnp.float32),
        ),
        in_specs=[pl.BlockSpec(memory_space=pltpu.HBM)] * 2,
        out_specs=(pl.BlockSpec(memory_space=pl.ANY),) * 2,
        scratch_shapes=[
            vmem(5, FIELD, LAYERS),
            vmem(FIELD, LAYERS),
            vmem(2, EXT),
            vmem(2, 2, 3),
            vmem(4, FIELD, LAYERS),
            vmem(4, FIELD, LAYERS),
            vmem(FIELD, LAYERS),
            vmem(FIELD, LAYERS + 2),
            vmem(2, 5, FIELD),
            vmem(5, FIELD, LAYERS),
            vmem(2, FIELD, 3),
            vmem(2, 5, FIELD),
            vmem(2, 5, FIELD),
            vmem(FIELD, LAYERS),
            vmem(2, 3),
            vmem(2, 2, 3),
            vmem(FIELD, LAYERS),
            vmem(4, 3),
            vmem(4, 3),
            vmem(4, FIELD, LAYERS),
            dma((4,)),
            dma((6,)),
            dma((3,)),
            dma((3,)),
            dma((2, 2)),
            dma((2, 2)),
            dma((2, 5)),
            dma((2, 5)),
            dma((2, 2)),
            dma((2, 2)),
            pltpu.SemaphoreType.REGULAR((2,)),
            pltpu.SemaphoreType.REGULAR((2,)),
        ],
        compiler_params=pltpu.CompilerParams(
            collective_id=0, has_side_effects=True, vmem_limit_bytes=54400 * 1024
        ),
    )(old_nodes, jnp.concatenate([initial, shear_modulus[None], mobility[None]], axis=0))


def solution(mesh):
    counts = (mesh.shape["tm"], mesh.shape["space"])
    return jax.shard_map(
        functools.partial(on_device, counts),
        mesh=mesh,
        in_specs=(
            P("tm", None, None, "space", None, None),
            P(None, "space", None, None),
            P("space", None, None),
            P("space", None, None),
        ),
        out_specs=(P("tm", None, None, "space", None, None), P("tm", None, "space", None, None)),
        check_vma=False,
    )
```

```python
import functools
import math

import jax
import jax.numpy as jnp
from jax import lax
from jax.experimental import pallas as pl
from jax.experimental.pallas import tpu as pltpu
from jax.sharding import PartitionSpec as P

MESH = pl.DeviceIdType.MESH
slice_step = 0.4
LAYERS = 6
EXT = 12
FIELD = 4


def node_tables():
    root_gap = math.sqrt(3.0 / 7.0)
    points = [0.0, (1.0 - root_gap) / 2.0, 0.5, (1.0 + root_gap) / 2.0, 1.0]
    polys = []
    for node in range(5):
        coeffs = [1.0]
        for other in range(5):
            if other != node:
                denom = points[node] - points[other]
                grown = [0.0] * (len(coeffs) + 1)
                for power in range(len(coeffs)):
                    grown[power + 1] += coeffs[power] / denom
                    grown[power] -= points[other] * coeffs[power] / denom
                coeffs = grown
        polys.append(coeffs)
    integral = []
    for column in range(4):
        lower = points[column]
        upper = points[column + 1]
        table_row = []
        for node in range(5):
            total = 0.0
            for power in range(5):
                total += (
                    polys[node][power] * (upper ** (power + 1) - lower ** (power + 1)) / (power + 1)
                )
            table_row.append(total * slice_step)
        integral.append(table_row)
    widths = [(points[column + 1] - points[column]) * slice_step for column in range(4)]
    return (integral, widths)


def positions(shape, axis):
    return lax.broadcasted_iota(jnp.int32, shape, axis)


def at(value, axis, step):
    size = value.shape[axis]
    moved = pltpu.roll(value, (-step) % size, axis)
    where = positions(value.shape, axis)
    inside = where < size - step if step > 0 else where >= -step
    return jnp.where(inside, moved, 0.0)


def operator(q, stiff, fluid, grad, step):
    out = [None] * 4
    diverge = None
    for k in (3, 0, 1, 2):
        center, below, above = q[k][1:-1], q[k][:-2], q[k][2:]
        xp, xm = at(center, 1, step), at(center, 1, -step)
        yp, ym = at(center, 2, step), at(center, 2, -step)
        laplace = ((xp + xm) + (yp + ym)) + (above + below) - 6.0 * center
        if k == 3:
            flow = fluid * laplace
            grads = [grad * (above - below), grad * (xp - xm), grad * (yp - ym)]
        else:
            out[k] = stiff * laplace - grads[k]
            part = (above - below, xp - xm, yp - ym)[k]
            diverge = part if diverge is None else diverge + part
    out[3] = flow - grad * diverge
    return out


def from_below(q, stiff, fluid, grad):
    return [stiff * q[0] + grad * q[3], stiff * q[1], stiff * q[2], fluid * q[3] + grad * q[0]]


def from_above(q, stiff, fluid, grad):
    return [stiff * q[0] - grad * q[3], stiff * q[1], stiff * q[2], fluid * q[3] - grad * q[0]]


def even(shape, axis):
    return positions(shape, axis) % 2 == 0


def pair_sums(a, b, axis):
    size = a.shape[axis]
    is_even = even(a.shape, axis)
    kept, other = jnp.where(is_even, a, b), jnp.where(is_even, b, a)
    return kept + jnp.where(is_even, pltpu.roll(other, size - 1, axis), pltpu.roll(other, 1, axis))


def means(q):
    return 0.125 * pair_sums(pair_sums(q[0], q[1], 2), pair_sums(q[2], q[3], 2), 1)


def layer_pairs(v):
    return jnp.concatenate([v[2 * i : 2 * i + 1] + v[2 * i + 1 : 2 * i + 2] for i in range(3)], axis=0)


def woven(q):
    shape = q[0].shape
    ye, xe = even(shape, 2), even(shape, 1)
    return jnp.where(xe, jnp.where(ye, q[0], q[1]), jnp.where(ye, q[2], q[3]))


def spread(p):
    ye, xe = even(p.shape, 2), even(p.shape, 1)
    a = jnp.where(ye, p, pltpu.roll(p, 1, 2))
    b = jnp.where(ye, pltpu.roll(p, 127, 2), p)
    return [
        jnp.where(xe, a, pltpu.roll(a, 1, 1)),
        jnp.where(xe, b, pltpu.roll(b, 1, 1)),
        jnp.where(xe, pltpu.roll(a, 7, 1), a),
        jnp.where(xe, pltpu.roll(b, 7, 1), b),
    ]


def twice(v):
    return jnp.concatenate([v[i // 2 : i // 2 + 1] for i in range(LAYERS)], axis=0)


def ends(v, low, high):
    return jnp.concatenate([v[:1] + low, v[1:-1], v[-1:] + high], axis=0)


def padded(v):
    zero = jnp.zeros_like(v[:1])
    return jnp.concatenate([zero, v, zero], axis=0)


def kernel(
    counts,
    old_hbm,
    rest_hbm,
    new_hbm,
    next_hbm,
    old,
    init,
    coef,
    coef_in,
    u,
    fu,
    start_in,
    primed,
    faces,
    node,
    halo,
    face_out,
    face_in,
    image,
    coarse_out,
    coarse_in,
    last_in,
    end_out,
    end_in,
    result,
    local_sem,
    write_sem,
    tm_send,
    tm_recv,
    coef_send,
    coef_recv,
    face_send,
    face_recv,
    coarse_send,
    coarse_recv,
    ready,
    later_ready,
):
    integral, widths = node_tables()
    table = [[integral[m][j] - (widths[m] if j == m else 0.0) for j in range(5)] for m in range(4)]
    slices, slabs = counts
    t, s = lax.axis_index("tm"), lax.axis_index("space")
    before, after = (lax.rem(t + slices - 1, slices), s), (lax.rem(t + 1, slices), s)
    below, above = (t, lax.rem(s + slabs - 1, slabs)), (t, lax.rem(s + 1, slabs))
    below_after, above_after = (after[0], below[1]), (after[0], above[1])
    has_below, has_above, has_before, has_after = s > 0, s < slabs - 1, t > 0, t < slices - 1
    exists = (has_below, has_above)

    place = lax.rem(s, 4)
    greets = (
        jnp.logical_or(place == 0, place == 3),
        jnp.logical_or(place == 0, place == 1),
    )
    leads = tuple(jnp.logical_and(exists[side], greets[side]) for side in range(2))
    follows = tuple(jnp.logical_and(exists[side], jnp.logical_not(greets[side])) for side in range(2))
    barrier = pltpu.get_barrier_semaphore()
    for wanted, device in ((has_before, before), (leads[0], below), (leads[1], above)):

        @pl.when(wanted)
        def _():
            pl.semaphore_signal(barrier, inc=1, device_id=device, device_id_type=MESH)

    loads = [
        pltpu.make_async_copy(old_hbm.at[0], old, local_sem.at[0]),
        pltpu.make_async_copy(rest_hbm.at[FIELD], coef.at[0, pl.ds(3, LAYERS)], local_sem.at[1]),
        pltpu.make_async_copy(rest_hbm.at[FIELD + 1], coef.at[1, pl.ds(3, LAYERS)], local_sem.at[2]),
        pltpu.make_async_copy(rest_hbm.at[pl.ds(0, FIELD)], init, local_sem.at[3]),
    ]
    for load in loads:
        load.start()
    for load in loads:
        load.wait()

    stiff, fluid = coef[0, 3 : 3 + LAYERS], coef[1, 3 : 3 + LAYERS]

    for m in range(4):
        for k in range(FIELD):
            total = table[m][0] * old[0, k]
            for j in range(1, 5):
                total = total + table[m][j] * old[j, k]
            u[m, k] = total
    for m in range(4):
        images = operator([padded(u[m, k]) for k in range(FIELD)], stiff, fluid, 0.25, 1)
        for k in range(FIELD):
            fu[m, k] = images[k]
        end_out[m] = means([layer_pairs(images[k]) for k in range(FIELD)])

    greeted = [jnp.where(c, 1, 0) for c in (has_after,) + follows]
    greeted = greeted[0] + greeted[1] + greeted[2]

    @pl.when(greeted > 0)
    def _():
        pl.semaphore_wait(barrier, greeted)

    def remote(src, dst, send, recv, device):
        return pltpu.make_async_remote_copy(
            src_ref=src, dst_ref=dst, send_sem=send, recv_sem=recv, device_id=device, device_id_type=MESH
        )

    def start_if(wanted, *copies):
        @pl.when(wanted)
        def _():
            for copy in copies:
                copy.start()

    def wait_if(wanted, *copies):
        @pl.when(wanted)
        def _():
            for copy in copies:
                copy.wait_recv()

    start_copy = remote(old.at[4], start_in, tm_send.at[0], tm_recv.at[0], after)
    start_if(has_after, start_copy)
    coef_copies = [
        remote(coef.at[:, pl.ds(3, 1)], coef_in.at[1, :, pl.ds(0, 1)], coef_send.at[0, 0], coef_recv.at[0, 1], below),
        remote(coef.at[:, pl.ds(8, 1)], coef_in.at[0, :, pl.ds(2, 1)], coef_send.at[0, 1], coef_recv.at[0, 0], above),
    ]
    deep_copies = [
        remote(coef.at[:, pl.ds(4, 1)], coef_in.at[1, :, pl.ds(1, 1)], coef_send.at[1, 0], coef_recv.at[1, 1], below),
        remote(coef.at[:, pl.ds(7, 1)], coef_in.at[0, :, pl.ds(1, 1)], coef_send.at[1, 1], coef_recv.at[1, 0], above),
    ]
    for side, device in ((0, below), (1, above)):

        @pl.when(follows[side])
        def _():
            pl.semaphore_signal(ready.at[1 - side], inc=1, device_id=device, device_id_type=MESH)
            coef_copies[side].start()
            deep_copies[side].start()

        @pl.when(jnp.logical_not(exists[side]))
        def _():
            face_in[side] = jnp.zeros((5, FIELD, 8, 128), jnp.float32)
            coef_in[side] = jnp.zeros((2, 3, 8, 128), jnp.float32)
            coarse_in[:, side] = jnp.zeros((2, 3, 8, 128), jnp.float32)

    @pl.when(jnp.logical_not(has_before))
    def _():
        start_in[...] = init[...]

    wait_if(has_before, start_copy)

    def pass_on(side):
        @pl.when(has_before)
        def _():
            pl.semaphore_signal(later_ready.at[side], inc=1, device_id=before, device_id_type=MESH)

    for side in range(2):

        @pl.when(follows[side])
        def _():
            pass_on(side)

    for k in range(FIELD):
        first = start_in[k]
        node[0, k] = first
        primed[k] = padded(first)
    writes = [pltpu.make_async_copy(node.at[0], new_hbm.at[0, 0], write_sem.at[0])]
    writes[0].start()

    face_copies = []
    for m in range(5):
        for side, layer in ((0, 0), (1, LAYERS - 1)):
            for k in range(FIELD):
                face = primed[k, layer + 1]
                faces[side, m, k] = face
                if m < 4:
                    face_out[side, m, k] = widths[m] * face + u[m, k, layer]
        if m == 4:
            break
        for side, device in ((0, below), (1, above)):
            copy = remote(
                face_out.at[side, m],
                face_in.at[1 - side, m],
                face_send.at[side, m],
                face_recv.at[1 - side, m],
                device,
            )
            start_if(follows[side], copy)
            face_copies.append(copy)
        images = operator([primed[k] for k in range(FIELD)], stiff, fluid, 0.25, 1)
        for k in range(FIELD):
            moved = primed[k, 1 : 1 + LAYERS] + widths[m] * images[k] + fu[m, k]
            primed[k, 1 : 1 + LAYERS] = moved
            if m == 0:
                node[1, k] = moved
                image[k] = images[k]

    for side in (1, 0):

        @pl.when(leads[side])
        def _():
            pl.semaphore_wait(ready.at[side], 1)
            coef_copies[side].start()
            face_copies[side].start()
            pass_on(side)
            face_copies[2 + side].start()
            deep_copies[side].start()
            face_copies[4 + side].start()
            face_copies[6 + side].start()

    for side in range(2):
        wait_if(exists[side], coef_copies[1 - side])
        for array in range(2):
            lo, layer = ((2, 2), (9, 0))[side]
            coef[array, lo : lo + 1] = coef_in[side, array, layer : layer + 1]
    gradients = [jnp.where(exists[side], 0.25, 0.0) for side in range(2)]

    def across(q, side):
        layer = (2, 9)[side]
        reach = (from_above, from_below)[side]
        return reach(q, coef[0, layer : layer + 1], coef[1, layer : layer + 1], gradients[side])

    for side in range(2):
        layer = (0, LAYERS - 1)[side]
        for m in range(4):
            z = []
            for k in range(FIELD):
                total = table[m][0] * faces[side, 0, k]
                for j in range(1, 5):
                    total = total + table[m][j] * faces[side, j, k]
                z.append((total - u[m, k, layer])[None])
            face_out[side, 4, m] = means(across(z, side))[0]
    for side, device in ((0, below), (1, above)):
        copy = remote(
            face_out.at[side, 4],
            face_in.at[1 - side, 4],
            face_send.at[side, 4],
            face_recv.at[1 - side, 4],
            device,
        )
        start_if(exists[side], copy)
        face_copies.append(copy)

    def inflow(side, m):
        layer = (3, 8)[side]
        q = [face_in[side, m, k][None] for k in range(FIELD)]
        reach = (from_below, from_above)[side]
        return reach(q, coef[0, layer : layer + 1], coef[1, layer : layer + 1], 0.25)

    def edge(m, side):
        return [u[m, k, (0, LAYERS - 1)[side]][None] for k in range(FIELD)]

    for side in range(2):
        wait_if(exists[side], face_copies[1 - side])
    low, high = inflow(0, 0), inflow(1, 0)
    zero = jnp.zeros((2, 8, 128), jnp.float32)
    out_low = across([face_out[0, 0, k][None] for k in range(FIELD)], 0)
    out_high = across([face_out[1, 0, k][None] for k in range(FIELD)], 1)
    for k in range(FIELD):
        node[1, k] = ends(node[1, k], low[k], high[k])
        halo[0, k] = jnp.concatenate([zero, out_low[k]], axis=0)
        halo[1, k] = jnp.concatenate([out_high[k], zero], axis=0)

    sums = [means([layer_pairs(image[k]) for k in range(FIELD)])]
    grad = jnp.concatenate(
        [
            jnp.full((3, 8, 128), 1.0, jnp.float32) * gradients[0],
            jnp.full((LAYERS, 8, 128), 0.25, jnp.float32),
            jnp.full((3, 8, 128), 1.0, jnp.float32) * gradients[1],
        ],
        axis=0,
    )
    for m in range(1, 5):
        if m == 1:
            for side in range(2):
                wait_if(exists[side], deep_copies[1 - side])
                for array in range(2):
                    lo = (1, 10)[side]
                    coef[array, lo : lo + 1] = coef_in[side, array, 1:2]
        reach = (0, 2, 2, 1, 0)[m]
        own = slice(reach, reach + LAYERS)
        lo, hi = 3 - reach, 9 + reach
        q = []
        for k in range(FIELD):
            q.append(
                jnp.concatenate([halo[0, k, 2 - reach :], node[m, k], halo[1, k, : reach + 1]], axis=0)
            )
        images = operator(q, coef[0, lo:hi], coef[1, lo:hi], grad[lo:hi], 1)
        sums.append(means([layer_pairs(images[k][own]) for k in range(FIELD)]))
        if m == 4:
            break
        for side in range(2):
            wait_if(exists[side], face_copies[2 * m + 1 - side])
        low, high = inflow(0, m), inflow(1, m)
        out_low, out_high = across(edge(m, 0), 0), across(edge(m, 1), 1)
        for k in range(FIELD):
            moved = node[m, k] + widths[m] * images[k][own] + fu[m, k]
            node[m + 1, k] = ends(moved, low[k], high[k])
            inner = halo[0, k, 3 - reach :] + widths[m] * images[k][:reach]
            halo[0, k, 3 - reach :] = jnp.concatenate([inner[:-1], inner[-1:] + out_low[k]], axis=0) if reach > 1 else inner + out_low[k]
            inner = halo[1, k, :reach] + widths[m] * images[k][reach + LAYERS :]
            halo[1, k, :reach] = jnp.concatenate([inner[:1] + out_high[k], inner[1:]], axis=0) if reach > 1 else inner + out_high[k]

    partial = []
    for m in range(4):
        total = table[m][0] * sums[0]
        for j in range(1, 5):
            total = total + table[m][j] * sums[j]
        partial.append(total - end_out[m])

    def coarse_coef(lo, pairs):
        both = [
            jnp.concatenate(
                [
                    coef[a, lo + 2 * i : lo + 2 * i + 1] + coef[a, lo + 2 * i + 1 : lo + 2 * i + 2]
                    for i in range(pairs)
                ],
                axis=0,
            )
            for a in range(2)
        ]
        pieces = spread(means([both[0], both[0], both[1], both[1]]))
        return 0.25 * pieces[0], 0.25 * pieces[2]

    coarse_stiff, coarse_fluid = coarse_coef(1, 5)
    weight = 0.5 * grad[2:10]
    coarse_grad = jnp.concatenate([weight[0:1], weight[1:4], weight[7:8]], axis=0)
    own_stiff, own_fluid = coarse_stiff[1:4], coarse_fluid[1:4]

    errors = []
    for side in range(2):
        wait_if(exists[side], face_copies[9 - side])
    for m in range(4):
        total = ends(partial[m], face_in[0, 4, m][None], face_in[1, 4, m][None])
        end_out[m] = total
        errors.append(spread(total))

    def sweep_alone(e):
        d = [[e[0][k] for k in range(FIELD)]]
        for m in (1, 2):
            images = operator([padded(v) for v in d[-1]], own_stiff, own_fluid, 0.125, 2)
            d.append([d[-1][k] + widths[m] * images[k] + e[m][k] for k in range(FIELD)])
        return d

    alone = sweep_alone(errors)
    for m in range(3):
        for side, layer in ((0, 0), (1, 2)):
            coarse_out[side, m] = woven([alone[m][k][layer : layer + 1] for k in range(FIELD)])[0]
    end_copies = [remote(end_out, end_in, tm_send.at[2], tm_recv.at[2], after)]
    coarse_copies = []
    for side, device, later in ((0, below, below_after), (1, above, above_after)):
        coarse_copies.append(
            remote(
                coarse_out.at[side],
                coarse_in.at[0, 1 - side],
                coarse_send.at[0, side],
                coarse_recv.at[0, 1 - side],
                device,
            )
        )
        end_copies.append(
            remote(
                coarse_out.at[side],
                coarse_in.at[1, 1 - side],
                coarse_send.at[1, side],
                coarse_recv.at[1, 1 - side],
                later,
            )
        )
    for side in range(2):
        start_if(exists[side], coarse_copies[side])
    last_copy = remote(node.at[4], last_in, tm_send.at[1], tm_recv.at[1], after)
    start_if(has_after, end_copies[0], last_copy)
    for side in range(2):

        @pl.when(jnp.logical_and(exists[side], has_after))
        def _():
            pl.semaphore_wait(later_ready.at[side], 1)
            end_copies[1 + side].start()

    def finish(m, d):
        for k in range(FIELD):
            result[m - 1, k] = node[m, k] + twice(d[k])
        write = pltpu.make_async_copy(result.at[m - 1], new_hbm.at[0, m], write_sem.at[m])
        write.start()
        writes.append(write)

    finish(1, alone[0])

    def coarse_across(q, side):
        layer = (0, 4)[side]
        reach = (from_above, from_below)[side]
        part = slice(layer, layer + 1)
        return reach(q, coarse_stiff[part], coarse_fluid[part], coarse_grad[part])

    def sweep(e, d, slot, arrivals):
        d1, d2 = d[0], d[1]
        halo_low = [widths[1] * v for v in coarse_across([v[0:1] for v in d1], 0)]
        halo_high = [widths[1] * v for v in coarse_across([v[2:3] for v in d1], 1)]
        for side in range(2):
            wait_if(exists[side], arrivals[1 - side])
        coming = [
            [spread(coarse_in[slot, side, m][None]) for m in range(3)]
            for side in range(2)
        ]

        def coarse_inflow(m):
            low = from_below(coming[0][m], own_stiff[0:1], own_fluid[0:1], 0.125)
            high = from_above(coming[1][m], own_stiff[2:3], own_fluid[2:3], 0.125)
            return low, high

        low, high = coarse_inflow(0)
        d2 = [ends(d2[k], widths[1] * low[k], widths[1] * high[k]) for k in range(FIELD)]
        low, high = coarse_inflow(1)
        q = [padded(jnp.concatenate([halo_low[k], d2[k], halo_high[k]], axis=0)) for k in range(FIELD)]
        images = operator(q, coarse_stiff, coarse_fluid, coarse_grad, 2)
        d3 = [
            d2[k] + widths[2] * ends(images[k][1:4], low[k], high[k]) + e[2][k] for k in range(FIELD)
        ]
        halo_low = [halo_low[k] + widths[2] * images[k][0:1] for k in range(FIELD)]
        halo_high = [halo_high[k] + widths[2] * images[k][4:5] for k in range(FIELD)]
        halo_low = [halo_low[k] + coming[0][2][k] for k in range(FIELD)]
        halo_high = [halo_high[k] + coming[1][2][k] for k in range(FIELD)]
        q = [jnp.concatenate([halo_low[k], d3[k], halo_high[k]], axis=0) for k in range(FIELD)]
        images = operator(q, own_stiff, own_fluid, 0.125, 2)
        d4 = [d3[k] + widths[3] * images[k] + e[3][k] for k in range(FIELD)]
        return d2, d3, d4

    d2, d3, d4 = sweep(errors, alone, 0, coarse_copies)
    finish(2, d2)
    finish(3, d3)
    finish(4, d4)

    @pl.when(has_before)
    def _():
        end_copies[0].wait_recv()
        errors = [spread(end_in[m]) for m in range(4)]
        d4 = sweep(errors, sweep_alone(errors), 1, end_copies[1:])[2]
        last_copy.wait_recv()
        for k in range(FIELD):
            start_in[k] = last_in[k] + twice(d4[k])

    write = pltpu.make_async_copy(start_in, next_hbm.at[0], write_sem.at[5])
    write.start()
    writes.append(write)

    def sent_if(wanted, *copies):
        @pl.when(wanted)
        def _():
            for copy in copies:
                copy.wait_send()

    sent_if(has_after, start_copy, last_copy, end_copies[0])
    for side in range(2):
        sent_if(exists[side], coef_copies[side], deep_copies[side], coarse_copies[side], *face_copies[side::2])
        sent_if(jnp.logical_and(exists[side], has_after), end_copies[1 + side])
    for write in writes:
        write.wait()


def on_device(counts, old_nodes, initial, shear_modulus, mobility):
    def vmem(*shape):
        return pltpu.VMEM(shape + (8, 128), jnp.float32)

    dma = pltpu.SemaphoreType.DMA
    return pl.pallas_call(
        functools.partial(kernel, counts),
        out_shape=(
            jax.ShapeDtypeStruct((1, 5, FIELD, LAYERS, 8, 128), jnp.float32),
            jax.ShapeDtypeStruct((1, FIELD, LAYERS, 8, 128), jnp.float32),
        ),
        in_specs=[pl.BlockSpec(memory_space=pltpu.HBM)] * 2,
        out_specs=(pl.BlockSpec(memory_space=pl.ANY),) * 2,
        scratch_shapes=[
            vmem(5, FIELD, LAYERS),
            vmem(FIELD, LAYERS),
            vmem(2, EXT),
            vmem(2, 2, 3),
            vmem(4, FIELD, LAYERS),
            vmem(4, FIELD, LAYERS),
            vmem(FIELD, LAYERS),
            vmem(FIELD, LAYERS + 2),
            vmem(2, 5, FIELD),
            vmem(5, FIELD, LAYERS),
            vmem(2, FIELD, 3),
            vmem(2, 5, FIELD),
            vmem(2, 5, FIELD),
            vmem(FIELD, LAYERS),
            vmem(2, 3),
            vmem(2, 2, 3),
            vmem(FIELD, LAYERS),
            vmem(4, 3),
            vmem(4, 3),
            vmem(4, FIELD, LAYERS),
            dma((4,)),
            dma((6,)),
            dma((3,)),
            dma((3,)),
            dma((2, 2)),
            dma((2, 2)),
            dma((2, 5)),
            dma((2, 5)),
            dma((2, 2)),
            dma((2, 2)),
            pltpu.SemaphoreType.REGULAR((2,)),
            pltpu.SemaphoreType.REGULAR((2,)),
        ],
        compiler_params=pltpu.CompilerParams(
            collective_id=0, has_side_effects=True, vmem_limit_bytes=54400 * 1024
        ),
    )(old_nodes, jnp.concatenate([initial, shear_modulus[None], mobility[None]], axis=0))


def solution(mesh):
    counts = (mesh.shape["tm"], mesh.shape["space"])
    return jax.shard_map(
        functools.partial(on_device, counts),
        mesh=mesh,
        in_specs=(
            P("tm", None, None, "space", None, None),
            P(None, "space", None, None),
            P("space", None, None),
            P("space", None, None),
        ),
        out_specs=(P("tm", None, None, "space", None, None), P("tm", None, "space", None, None)),
        check_vma=False,
    )
```

```python
import functools
import math

import jax
import jax.numpy as jnp
from jax import lax
from jax.experimental import pallas as pl
from jax.experimental.pallas import tpu as pltpu
from jax.sharding import PartitionSpec as P

MESH = pl.DeviceIdType.MESH
slice_step = 0.4
LAYERS = 6
EXT = 12
FIELD = 4


def node_tables():
    root_gap = math.sqrt(3.0 / 7.0)
    points = [0.0, (1.0 - root_gap) / 2.0, 0.5, (1.0 + root_gap) / 2.0, 1.0]
    polys = []
    for node in range(5):
        coeffs = [1.0]
        for other in range(5):
            if other != node:
                denom = points[node] - points[other]
                grown = [0.0] * (len(coeffs) + 1)
                for power in range(len(coeffs)):
                    grown[power + 1] += coeffs[power] / denom
                    grown[power] -= points[other] * coeffs[power] / denom
                coeffs = grown
        polys.append(coeffs)
    integral = []
    for column in range(4):
        lower = points[column]
        upper = points[column + 1]
        table_row = []
        for node in range(5):
            total = 0.0
            for power in range(5):
                total += (
                    polys[node][power] * (upper ** (power + 1) - lower ** (power + 1)) / (power + 1)
                )
            table_row.append(total * slice_step)
        integral.append(table_row)
    widths = [(points[column + 1] - points[column]) * slice_step for column in range(4)]
    return (integral, widths)


def positions(shape, axis):
    return lax.broadcasted_iota(jnp.int32, shape, axis)


def at(value, axis, step):
    size = value.shape[axis]
    moved = pltpu.roll(value, (-step) % size, axis)
    where = positions(value.shape, axis)
    inside = where < size - step if step > 0 else where >= -step
    return jnp.where(inside, moved, 0.0)


def operator(q, stiff, fluid, grad, step):
    out = [None] * 4
    diverge = None
    for k in (3, 0, 1, 2):
        center, below, above = q[k][1:-1], q[k][:-2], q[k][2:]
        xp, xm = at(center, 1, step), at(center, 1, -step)
        yp, ym = at(center, 2, step), at(center, 2, -step)
        laplace = ((xp + xm) + (yp + ym)) + (above + below) - 6.0 * center
        if k == 3:
            flow = fluid * laplace
            grads = [grad * (above - below), grad * (xp - xm), grad * (yp - ym)]
        else:
            out[k] = stiff * laplace - grads[k]
            part = (above - below, xp - xm, yp - ym)[k]
            diverge = part if diverge is None else diverge + part
    out[3] = flow - grad * diverge
    return out


def from_below(q, stiff, fluid, grad):
    return [stiff * q[0] + grad * q[3], stiff * q[1], stiff * q[2], fluid * q[3] + grad * q[0]]


def from_above(q, stiff, fluid, grad):
    return [stiff * q[0] - grad * q[3], stiff * q[1], stiff * q[2], fluid * q[3] - grad * q[0]]


def even(shape, axis):
    return positions(shape, axis) % 2 == 0


def pair_sums(a, b, axis):
    size = a.shape[axis]
    is_even = even(a.shape, axis)
    kept, other = jnp.where(is_even, a, b), jnp.where(is_even, b, a)
    return kept + jnp.where(is_even, pltpu.roll(other, size - 1, axis), pltpu.roll(other, 1, axis))


def means(q):
    return 0.125 * pair_sums(pair_sums(q[0], q[1], 2), pair_sums(q[2], q[3], 2), 1)


def layer_pairs(v):
    return jnp.concatenate([v[2 * i : 2 * i + 1] + v[2 * i + 1 : 2 * i + 2] for i in range(3)], axis=0)


def woven(q):
    shape = q[0].shape
    ye, xe = even(shape, 2), even(shape, 1)
    return jnp.where(xe, jnp.where(ye, q[0], q[1]), jnp.where(ye, q[2], q[3]))


def spread(p):
    ye, xe = even(p.shape, 2), even(p.shape, 1)
    a = jnp.where(ye, p, pltpu.roll(p, 1, 2))
    b = jnp.where(ye, pltpu.roll(p, 127, 2), p)
    return [
        jnp.where(xe, a, pltpu.roll(a, 1, 1)),
        jnp.where(xe, b, pltpu.roll(b, 1, 1)),
        jnp.where(xe, pltpu.roll(a, 7, 1), a),
        jnp.where(xe, pltpu.roll(b, 7, 1), b),
    ]


def twice(v):
    return jnp.concatenate([v[i // 2 : i // 2 + 1] for i in range(LAYERS)], axis=0)


def ends(v, low, high):
    return jnp.concatenate([v[:1] + low, v[1:-1], v[-1:] + high], axis=0)


def padded(v):
    zero = jnp.zeros_like(v[:1])
    return jnp.concatenate([zero, v, zero], axis=0)


def kernel(
    counts,
    old_hbm,
    rest_hbm,
    new_hbm,
    next_hbm,
    old,
    init,
    coef,
    coef_in,
    u,
    fu,
    start_in,
    primed,
    faces,
    node,
    halo,
    face_out,
    face_in,
    image,
    coarse_out,
    coarse_in,
    last_in,
    end_out,
    end_in,
    result,
    local_sem,
    write_sem,
    tm_send,
    tm_recv,
    coef_send,
    coef_recv,
    face_send,
    face_recv,
    coarse_send,
    coarse_recv,
    ready,
    later_ready,
):
    integral, widths = node_tables()
    table = [[integral[m][j] - (widths[m] if j == m else 0.0) for j in range(5)] for m in range(4)]
    slices, slabs = counts
    t, s = lax.axis_index("tm"), lax.axis_index("space")
    before, after = (lax.rem(t + slices - 1, slices), s), (lax.rem(t + 1, slices), s)
    below, above = (t, lax.rem(s + slabs - 1, slabs)), (t, lax.rem(s + 1, slabs))
    below_after, above_after = (after[0], below[1]), (after[0], above[1])
    has_below, has_above, has_before, has_after = s > 0, s < slabs - 1, t > 0, t < slices - 1
    exists = (has_below, has_above)

    place = lax.rem(s, 4)
    greets = (
        jnp.logical_or(place == 0, place == 3),
        jnp.logical_or(place == 0, place == 1),
    )
    leads = tuple(jnp.logical_and(exists[side], greets[side]) for side in range(2))
    follows = tuple(jnp.logical_and(exists[side], jnp.logical_not(greets[side])) for side in range(2))
    barrier = pltpu.get_barrier_semaphore()
    for wanted, device in ((has_before, before), (leads[0], below), (leads[1], above)):

        @pl.when(wanted)
        def _():
            pl.semaphore_signal(barrier, inc=1, device_id=device, device_id_type=MESH)

    loads = [
        pltpu.make_async_copy(old_hbm.at[0], old, local_sem.at[0]),
        pltpu.make_async_copy(rest_hbm.at[FIELD], coef.at[0, pl.ds(3, LAYERS)], local_sem.at[1]),
        pltpu.make_async_copy(rest_hbm.at[FIELD + 1], coef.at[1, pl.ds(3, LAYERS)], local_sem.at[2]),
        pltpu.make_async_copy(rest_hbm.at[pl.ds(0, FIELD)], init, local_sem.at[3]),
    ]
    for load in loads:
        load.start()
    for load in loads:
        load.wait()

    stiff, fluid = coef[0, 3 : 3 + LAYERS], coef[1, 3 : 3 + LAYERS]

    for m in range(4):
        for k in range(FIELD):
            total = table[m][0] * old[0, k]
            for j in range(1, 5):
                total = total + table[m][j] * old[j, k]
            u[m, k] = total
    for m in range(4):
        images = operator([padded(u[m, k]) for k in range(FIELD)], stiff, fluid, 0.25, 1)
        for k in range(FIELD):
            fu[m, k] = images[k]
        end_out[m] = means([layer_pairs(images[k]) for k in range(FIELD)])

    greeted = [jnp.where(c, 1, 0) for c in (has_after,) + follows]
    greeted = greeted[0] + greeted[1] + greeted[2]

    @pl.when(greeted > 0)
    def _():
        pl.semaphore_wait(barrier, greeted)

    def remote(src, dst, send, recv, device):
        return pltpu.make_async_remote_copy(
            src_ref=src, dst_ref=dst, send_sem=send, recv_sem=recv, device_id=device, device_id_type=MESH
        )

    def start_if(wanted, *copies):
        @pl.when(wanted)
        def _():
            for copy in copies:
                copy.start()

    def wait_if(wanted, *copies):
        @pl.when(wanted)
        def _():
            for copy in copies:
                copy.wait_recv()

    start_copy = remote(old.at[4], start_in, tm_send.at[0], tm_recv.at[0], after)
    start_if(has_after, start_copy)
    coef_copies = [
        remote(coef.at[:, pl.ds(3, 1)], coef_in.at[1, :, pl.ds(0, 1)], coef_send.at[0, 0], coef_recv.at[0, 1], below),
        remote(coef.at[:, pl.ds(8, 1)], coef_in.at[0, :, pl.ds(2, 1)], coef_send.at[0, 1], coef_recv.at[0, 0], above),
    ]
    deep_copies = [
        remote(coef.at[:, pl.ds(4, 1)], coef_in.at[1, :, pl.ds(1, 1)], coef_send.at[1, 0], coef_recv.at[1, 1], below),
        remote(coef.at[:, pl.ds(7, 1)], coef_in.at[0, :, pl.ds(1, 1)], coef_send.at[1, 1], coef_recv.at[1, 0], above),
    ]
    for side, device in ((0, below), (1, above)):

        @pl.when(follows[side])
        def _():
            pl.semaphore_signal(ready.at[1 - side], inc=1, device_id=device, device_id_type=MESH)
            coef_copies[side].start()
            deep_copies[side].start()

        @pl.when(jnp.logical_not(exists[side]))
        def _():
            face_in[side] = jnp.zeros((5, FIELD, 8, 128), jnp.float32)
            coef_in[side] = jnp.zeros((2, 3, 8, 128), jnp.float32)
            coarse_in[:, side] = jnp.zeros((2, 3, 8, 128), jnp.float32)

    @pl.when(jnp.logical_not(has_before))
    def _():
        start_in[...] = init[...]

    wait_if(has_before, start_copy)

    def pass_on(side):
        @pl.when(has_before)
        def _():
            pl.semaphore_signal(later_ready.at[side], inc=1, device_id=before, device_id_type=MESH)

    for side in range(2):

        @pl.when(follows[side])
        def _():
            pass_on(side)

    for k in range(FIELD):
        first = start_in[k]
        node[0, k] = first
        primed[k] = padded(first)
    writes = [pltpu.make_async_copy(node.at[0], new_hbm.at[0, 0], write_sem.at[0])]
    writes[0].start()

    face_copies = []
    for m in range(5):
        for side, layer in ((0, 0), (1, LAYERS - 1)):
            for k in range(FIELD):
                face = primed[k, layer + 1]
                faces[side, m, k] = face
                if m < 4:
                    face_out[side, m, k] = widths[m] * face + u[m, k, layer]
        if m == 4:
            break
        for side, device in ((0, below), (1, above)):
            copy = remote(
                face_out.at[side, m],
                face_in.at[1 - side, m],
                face_send.at[side, m],
                face_recv.at[1 - side, m],
                device,
            )
            start_if(follows[side], copy)
            face_copies.append(copy)
        images = operator([primed[k] for k in range(FIELD)], stiff, fluid, 0.25, 1)
        for k in range(FIELD):
            moved = primed[k, 1 : 1 + LAYERS] + widths[m] * images[k] + fu[m, k]
            primed[k, 1 : 1 + LAYERS] = moved
            if m == 0:
                node[1, k] = moved
                image[k] = images[k]

    for side in (1, 0):

        @pl.when(leads[side])
        def _():
            pl.semaphore_wait(ready.at[side], 1)
            coef_copies[side].start()
            face_copies[side].start()
            pass_on(side)
            face_copies[2 + side].start()
            deep_copies[side].start()
            face_copies[4 + side].start()
            face_copies[6 + side].start()

    for side in range(2):
        wait_if(exists[side], coef_copies[1 - side])
        for array in range(2):
            lo, layer = ((2, 2), (9, 0))[side]
            coef[array, lo : lo + 1] = coef_in[side, array, layer : layer + 1]
    gradients = [jnp.where(exists[side], 0.25, 0.0) for side in range(2)]

    def across(q, side):
        layer = (2, 9)[side]
        reach = (from_above, from_below)[side]
        return reach(q, coef[0, layer : layer + 1], coef[1, layer : layer + 1], gradients[side])

    for side in range(2):
        layer = (0, LAYERS - 1)[side]
        for m in range(4):
            z = []
            for k in range(FIELD):
                total = table[m][0] * faces[side, 0, k]
                for j in range(1, 5):
                    total = total + table[m][j] * faces[side, j, k]
                z.append((total - u[m, k, layer])[None])
            face_out[side, 4, m] = means(across(z, side))[0]
    for side, device in ((0, below), (1, above)):
        copy = remote(
            face_out.at[side, 4],
            face_in.at[1 - side, 4],
            face_send.at[side, 4],
            face_recv.at[1 - side, 4],
            device,
        )
        start_if(exists[side], copy)
        face_copies.append(copy)

    def inflow(side, m):
        layer = (3, 8)[side]
        q = [face_in[side, m, k][None] for k in range(FIELD)]
        reach = (from_below, from_above)[side]
        return reach(q, coef[0, layer : layer + 1], coef[1, layer : layer + 1], 0.25)

    def edge(m, side):
        return [u[m, k, (0, LAYERS - 1)[side]][None] for k in range(FIELD)]

    for side in range(2):
        wait_if(exists[side], face_copies[1 - side])
    low, high = inflow(0, 0), inflow(1, 0)
    zero = jnp.zeros((2, 8, 128), jnp.float32)
    out_low = across([face_out[0, 0, k][None] for k in range(FIELD)], 0)
    out_high = across([face_out[1, 0, k][None] for k in range(FIELD)], 1)
    for k in range(FIELD):
        node[1, k] = ends(node[1, k], low[k], high[k])
        halo[0, k] = jnp.concatenate([zero, out_low[k]], axis=0)
        halo[1, k] = jnp.concatenate([out_high[k], zero], axis=0)

    sums = [means([layer_pairs(image[k]) for k in range(FIELD)])]
    grad = jnp.concatenate(
        [
            jnp.full((3, 8, 128), 1.0, jnp.float32) * gradients[0],
            jnp.full((LAYERS, 8, 128), 0.25, jnp.float32),
            jnp.full((3, 8, 128), 1.0, jnp.float32) * gradients[1],
        ],
        axis=0,
    )
    for m in range(1, 5):
        if m == 1:
            for side in range(2):
                wait_if(exists[side], deep_copies[1 - side])
                for array in range(2):
                    lo = (1, 10)[side]
                    coef[array, lo : lo + 1] = coef_in[side, array, 1:2]
        reach = (0, 2, 2, 1, 0)[m]
        own = slice(reach, reach + LAYERS)
        lo, hi = 3 - reach, 9 + reach
        q = []
        for k in range(FIELD):
            q.append(
                jnp.concatenate([halo[0, k, 2 - reach :], node[m, k], halo[1, k, : reach + 1]], axis=0)
            )
        images = operator(q, coef[0, lo:hi], coef[1, lo:hi], grad[lo:hi], 1)
        sums.append(means([layer_pairs(images[k][own]) for k in range(FIELD)]))
        if m == 4:
            break
        for side in range(2):
            wait_if(exists[side], face_copies[2 * m + 1 - side])
        low, high = inflow(0, m), inflow(1, m)
        out_low, out_high = across(edge(m, 0), 0), across(edge(m, 1), 1)
        for k in range(FIELD):
            moved = node[m, k] + widths[m] * images[k][own] + fu[m, k]
            node[m + 1, k] = ends(moved, low[k], high[k])
            inner = halo[0, k, 3 - reach :] + widths[m] * images[k][:reach]
            halo[0, k, 3 - reach :] = jnp.concatenate([inner[:-1], inner[-1:] + out_low[k]], axis=0) if reach > 1 else inner + out_low[k]
            inner = halo[1, k, :reach] + widths[m] * images[k][reach + LAYERS :]
            halo[1, k, :reach] = jnp.concatenate([inner[:1] + out_high[k], inner[1:]], axis=0) if reach > 1 else inner + out_high[k]

    partial = []
    for m in range(4):
        total = table[m][0] * sums[0]
        for j in range(1, 5):
            total = total + table[m][j] * sums[j]
        partial.append(total - end_out[m])

    def coarse_coef(lo, pairs):
        both = [
            jnp.concatenate(
                [
                    coef[a, lo + 2 * i : lo + 2 * i + 1] + coef[a, lo + 2 * i + 1 : lo + 2 * i + 2]
                    for i in range(pairs)
                ],
                axis=0,
            )
            for a in range(2)
        ]
        pieces = spread(means([both[0], both[0], both[1], both[1]]))
        return 0.25 * pieces[0], 0.25 * pieces[2]

    coarse_stiff, coarse_fluid = coarse_coef(1, 5)
    weight = 0.5 * grad[2:10]
    coarse_grad = jnp.concatenate([weight[0:1], weight[1:4], weight[7:8]], axis=0)
    own_stiff, own_fluid = coarse_stiff[1:4], coarse_fluid[1:4]

    errors = []
    for side in range(2):
        wait_if(exists[side], face_copies[9 - side])
    for m in range(4):
        total = ends(partial[m], face_in[0, 4, m][None], face_in[1, 4, m][None])
        end_out[m] = total
        errors.append(spread(total))

    def sweep_alone(e):
        d = [[e[0][k] for k in range(FIELD)]]
        for m in (1, 2):
            images = operator([padded(v) for v in d[-1]], own_stiff, own_fluid, 0.125, 2)
            d.append([d[-1][k] + widths[m] * images[k] + e[m][k] for k in range(FIELD)])
        return d

    alone = sweep_alone(errors)
    for m in range(3):
        for side, layer in ((0, 0), (1, 2)):
            coarse_out[side, m] = woven([alone[m][k][layer : layer + 1] for k in range(FIELD)])[0]
    end_copies = [remote(end_out, end_in, tm_send.at[2], tm_recv.at[2], after)]
    coarse_copies = []
    for side, device, later in ((0, below, below_after), (1, above, above_after)):
        coarse_copies.append(
            remote(
                coarse_out.at[side],
                coarse_in.at[0, 1 - side],
                coarse_send.at[0, side],
                coarse_recv.at[0, 1 - side],
                device,
            )
        )
        end_copies.append(
            remote(
                coarse_out.at[side],
                coarse_in.at[1, 1 - side],
                coarse_send.at[1, side],
                coarse_recv.at[1, 1 - side],
                later,
            )
        )
    for side in range(2):
        start_if(exists[side], coarse_copies[side])
    start_if(has_after, end_copies[0])
    for side in range(2):

        @pl.when(jnp.logical_and(exists[side], has_after))
        def _():
            pl.semaphore_wait(later_ready.at[side], 1)
            end_copies[1 + side].start()

    def finish(m, d):
        for k in range(FIELD):
            result[m - 1, k] = node[m, k] + twice(d[k])
        write = pltpu.make_async_copy(result.at[m - 1], new_hbm.at[0, m], write_sem.at[m])
        write.start()
        writes.append(write)

    finish(1, alone[0])

    def coarse_across(q, side):
        layer = (0, 4)[side]
        reach = (from_above, from_below)[side]
        part = slice(layer, layer + 1)
        return reach(q, coarse_stiff[part], coarse_fluid[part], coarse_grad[part])

    def sweep(e, d, slot, arrivals):
        d1, d2 = d[0], d[1]
        halo_low = [widths[1] * v for v in coarse_across([v[0:1] for v in d1], 0)]
        halo_high = [widths[1] * v for v in coarse_across([v[2:3] for v in d1], 1)]
        for side in range(2):
            wait_if(exists[side], arrivals[1 - side])
        coming = [
            [spread(coarse_in[slot, side, m][None]) for m in range(3)]
            for side in range(2)
        ]

        def coarse_inflow(m):
            low = from_below(coming[0][m], own_stiff[0:1], own_fluid[0:1], 0.125)
            high = from_above(coming[1][m], own_stiff[2:3], own_fluid[2:3], 0.125)
            return low, high

        low, high = coarse_inflow(0)
        d2 = [ends(d2[k], widths[1] * low[k], widths[1] * high[k]) for k in range(FIELD)]
        low, high = coarse_inflow(1)
        q = [padded(jnp.concatenate([halo_low[k], d2[k], halo_high[k]], axis=0)) for k in range(FIELD)]
        images = operator(q, coarse_stiff, coarse_fluid, coarse_grad, 2)
        d3 = [
            d2[k] + widths[2] * ends(images[k][1:4], low[k], high[k]) + e[2][k] for k in range(FIELD)
        ]
        halo_low = [halo_low[k] + widths[2] * images[k][0:1] for k in range(FIELD)]
        halo_high = [halo_high[k] + widths[2] * images[k][4:5] for k in range(FIELD)]
        halo_low = [halo_low[k] + coming[0][2][k] for k in range(FIELD)]
        halo_high = [halo_high[k] + coming[1][2][k] for k in range(FIELD)]
        q = [jnp.concatenate([halo_low[k], d3[k], halo_high[k]], axis=0) for k in range(FIELD)]
        images = operator(q, own_stiff, own_fluid, 0.125, 2)
        d4 = [d3[k] + widths[3] * images[k] + e[3][k] for k in range(FIELD)]
        return d2, d3, d4

    last_copy = remote(node.at[4], last_in, tm_send.at[1], tm_recv.at[1], after)
    start_if(has_after, last_copy)
    d2, d3, d4 = sweep(errors, alone, 0, coarse_copies)
    finish(2, d2)
    finish(3, d3)
    finish(4, d4)

    @pl.when(has_before)
    def _():
        end_copies[0].wait_recv()
        errors = [spread(end_in[m]) for m in range(4)]
        d4 = sweep(errors, sweep_alone(errors), 1, end_copies[1:])[2]
        last_copy.wait_recv()
        for k in range(FIELD):
            start_in[k] = last_in[k] + twice(d4[k])

    write = pltpu.make_async_copy(start_in, next_hbm.at[0], write_sem.at[5])
    write.start()
    writes.append(write)

    def sent_if(wanted, *copies):
        @pl.when(wanted)
        def _():
            for copy in copies:
                copy.wait_send()

    sent_if(has_after, start_copy, last_copy, end_copies[0])
    for side in range(2):
        sent_if(exists[side], coef_copies[side], deep_copies[side], coarse_copies[side], *face_copies[side::2])
        sent_if(jnp.logical_and(exists[side], has_after), end_copies[1 + side])
    for write in writes:
        write.wait()


def on_device(counts, old_nodes, initial, shear_modulus, mobility):
    def vmem(*shape):
        return pltpu.VMEM(shape + (8, 128), jnp.float32)

    dma = pltpu.SemaphoreType.DMA
    return pl.pallas_call(
        functools.partial(kernel, counts),
        out_shape=(
            jax.ShapeDtypeStruct((1, 5, FIELD, LAYERS, 8, 128), jnp.float32),
            jax.ShapeDtypeStruct((1, FIELD, LAYERS, 8, 128), jnp.float32),
        ),
        in_specs=[pl.BlockSpec(memory_space=pltpu.HBM)] * 2,
        out_specs=(pl.BlockSpec(memory_space=pl.ANY),) * 2,
        scratch_shapes=[
            vmem(5, FIELD, LAYERS),
            vmem(FIELD, LAYERS),
            vmem(2, EXT),
            vmem(2, 2, 3),
            vmem(4, FIELD, LAYERS),
            vmem(4, FIELD, LAYERS),
            vmem(FIELD, LAYERS),
            vmem(FIELD, LAYERS + 2),
            vmem(2, 5, FIELD),
            vmem(5, FIELD, LAYERS),
            vmem(2, FIELD, 3),
            vmem(2, 5, FIELD),
            vmem(2, 5, FIELD),
            vmem(FIELD, LAYERS),
            vmem(2, 3),
            vmem(2, 2, 3),
            vmem(FIELD, LAYERS),
            vmem(4, 3),
            vmem(4, 3),
            vmem(4, FIELD, LAYERS),
            dma((4,)),
            dma((6,)),
            dma((3,)),
            dma((3,)),
            dma((2, 2)),
            dma((2, 2)),
            dma((2, 5)),
            dma((2, 5)),
            dma((2, 2)),
            dma((2, 2)),
            pltpu.SemaphoreType.REGULAR((2,)),
            pltpu.SemaphoreType.REGULAR((2,)),
        ],
        compiler_params=pltpu.CompilerParams(
            collective_id=0, has_side_effects=True, vmem_limit_bytes=54400 * 1024
        ),
    )(old_nodes, jnp.concatenate([initial, shear_modulus[None], mobility[None]], axis=0))


def solution(mesh):
    counts = (mesh.shape["tm"], mesh.shape["space"])
    return jax.shard_map(
        functools.partial(on_device, counts),
        mesh=mesh,
        in_specs=(
            P("tm", None, None, "space", None, None),
            P(None, "space", None, None),
            P("space", None, None),
            P("space", None, None),
        ),
        out_specs=(P("tm", None, None, "space", None, None), P("tm", None, "space", None, None)),
        check_vma=False,
    )
```
